32 devices in a mesh: groups: 2 (over y), seq: 4 (over z), tensor: 2 (over x), pipe: 2 (over core).
Axes of the slice: x: 2, y: 2, z: 4, core: 2. Of those that a mesh axis runs over, the one named last changes fastest.
Arguments:
- out_grad: bfloat16 [4, 1536, 3072], P(('groups', 'pipe'), 'seq', 'tensor'), parts along dimension 0, may hold values from -6 to 6
- queries: bfloat16 [4, 1536, 3072], P(('groups', 'pipe'), 'seq', 'tensor'), parts along dimension 0, may hold values from -0.3 to 0.3
- keys: bfloat16 [4, 1536, 3072], P(('groups', 'pipe'), 'seq', 'tensor'), parts along dimension 0, may hold values from -0.45 to 0.45
- main_out: bfloat16 [4, 512, 3072], P(('groups', 'pipe'), 'seq', 'tensor'), parts along dimension 0, may hold values from -6 to 6
- main_in_grad: bfloat16 [4, 512, 3072], P(('groups', 'pipe'), 'seq', 'tensor'), parts along dimension 0, may hold values from -6 to 6
- boundaries: int32 [4, 512], P(('groups', 'pipe')), parts along dimension 0, may hold values from 0 to 1535, as said below
- query_weight: bfloat16 [3072, 3072], P('seq', 'tensor'), may hold values from -0.109375 to 0.109375
- key_weight: bfloat16 [3072, 3072], P('seq', 'tensor'), may hold values from -0.109375 to 0.109375
Outputs:
- byte_grad: bfloat16 [4, 1536, 3072], P(('groups', 'pipe'), 'seq', 'tensor'), parts along dimension 0
- main_grad: bfloat16 [4, 512, 3072], P(('groups', 'pipe'), 'seq', 'tensor'), parts along dimension 0
The draws below stay inside these ranges and needn't reach their ends.
There are 2 independent parts, one for each index of `groups`. The reference program is written for one: setup_inputs(seed, part) draws one part's arguments, and reference() takes and returns one part's arrays. A program takes and returns all parts, laid end to end along the dimension named above; an argument that names none is the same for every part. Nothing has to cross between parts.
Inputs may be any that keep to these rules, and one draw needn't show every extreme that they name: `boundaries`: each row holds 512 strictly increasing byte positions, the first 0. Every span c that holds a byte of shard i (bytes i * 384 to (i + 1) * 384 - 1) has c // 128 within 2 of i, and in every sequence some span is exactly 2 away.
All inputs are finite; a program needn't handle non-finite values.
Results may differ from the reference program's by a relative error of at most 0.008.
Values may be sent and summed in bfloat16 or wider, within the bound.
No kernel may reach another device: no remote copies, remote signals or barrier semaphores. Data moves between devices by JAX's collectives and lax.ppermute only.
A program may use at most 128 MiB of HBM per device.

```python
import jax
import jax.numpy as jnp
from jax import lax

D = 3072
B_DEV = 384
SPAN_DEV = 128
SEQS = 2
SEQ_LEN = 1536
SPANS = 512
N_SEQ = 4
N_TENSOR = 2


def one_sequence(seed_key):
    key_heavy, key_drift, key_scores = jax.random.split(seed_key, 3)
    index = jnp.arange(N_SEQ, dtype=jnp.int32)
    heavy_shard = jax.random.randint(key_heavy, (), 0, N_SEQ - 2)
    drift = jax.random.randint(key_drift, (N_SEQ,), -(SPAN_DEV // 16), SPAN_DEV // 16 + 1)
    drift = jnp.where(index == N_SEQ - 1, 0, drift)
    earlier = jnp.concatenate([jnp.zeros((1,), jnp.int32), drift[:-1]])
    shed_rows = 3 * SPAN_DEV // 4
    surplus = jnp.where(index == heavy_shard, 2 * shed_rows, 0) - jnp.where((index == heavy_shard + 1) | (index == heavy_shard + 2), shed_rows, 0)
    counts = SPAN_DEV + drift - earlier + surplus
    columns = jnp.arange(B_DEV, dtype=jnp.int32)
    scores = jax.random.randint(key_scores, (N_SEQ, B_DEV), 0, 1 << 16) * B_DEV + columns[None, :]
    scores = jnp.where((index[:, None] == 0) & (columns[None, :] == 0), -1, scores)
    ranking = jnp.argsort(jnp.argsort(scores, axis=1), axis=1)
    chosen = ranking < counts[:, None]
    return jnp.nonzero(chosen.reshape(-1), size=SPANS)[0].astype(jnp.int32)


def draw_boundaries(key, part):
    key = jax.random.fold_in(key, 7)
    rows_all = []
    for sequence in range(SEQS):
        rows_all.append(one_sequence(jax.random.fold_in(key, sequence)))
    return jnp.stack(rows_all)


def clipped_normal(seed_key, shape):
    return jnp.clip(jax.random.normal(seed_key, shape, jnp.float32), -6.0, 6.0)


def column_place():
    return jnp.arange(D, dtype=jnp.float32) / (D - 1.0)


def query_values(seed_key, spread, ramp, rho_low, rho_high):
    key_base, key_rows, key_cols, key_rho = jax.random.split(seed_key, 4)
    base = clipped_normal(key_base, (SEQS, SEQ_LEN, D))
    shaped = base
    row_unit = jax.random.uniform(key_rows, (SEQS, SEQ_LEN), jnp.float32)
    col_unit = jax.random.uniform(key_cols, (D,), jnp.float32)
    row_scale = spread ** (2.0 * row_unit - 1.0)
    col_scale = spread ** (2.0 * col_unit - 1.0) * ramp ** (column_place() - 0.5)
    query_field = 0.02 * shaped * row_scale[:, :, None] * col_scale[None, None, :]
    rho_unit = jax.random.uniform(key_rho, (SEQS, SEQ_LEN), jnp.float32)
    rho_field = rho_low + (rho_high - rho_low) * rho_unit
    return (query_field, rho_field, col_scale)


def draw_queries(key, part):
    query_field, rho_field, col_scale = query_values(key, 1.0, 3.0, -0.9, 0.95)
    return query_field.astype(jnp.bfloat16)


def draw_keys(key, part):
    query_field, rho_field, col_scale = query_values(key, 1.0, 3.0, -0.9, 0.95)
    key = jax.random.fold_in(key, 11)
    key_noise = jax.random.fold_in(key, 0)
    noise = clipped_normal(key_noise, (SEQS, SEQ_LEN, D))
    noise = 0.02 * noise * col_scale[None, None, :]
    next_query = jnp.concatenate([query_field[:, 1:], jnp.zeros((SEQS, 1, D), jnp.float32)], 1)
    next_rho = jnp.concatenate([rho_field[:, 1:], jnp.zeros((SEQS, 1), jnp.float32)], 1)
    profile = 0.2 + 0.8 * column_place()
    rho_wide = next_rho[:, :, None] * profile[None, None, :]
    mixing = jnp.sqrt(1.0 - rho_wide * rho_wide)
    return (rho_wide * next_query + mixing * noise).astype(jnp.bfloat16)


def shard_levels(rng, extent, shards, smallest, largest):
    level, own = 1.0, jax.random.fold_in(rng, 6)
    for position, parts in shards:
        heights = jnp.exp(jax.random.uniform(jax.random.fold_in(own, position), (parts,), jnp.float32, smallest / len(shards), largest / len(shards)))
        level = level * jnp.repeat(heights, extent[position] // parts).reshape([-1 if axis == position else 1 for axis in range(len(extent))])
    return level


def centred(key, shape, scale, bound, cuts=(), held_as=jnp.bfloat16):
    values = scale * jax.random.normal(key, shape, jnp.float32)
    if cuts:
        values = values * shard_levels(key, shape, cuts, -0.22, 0.18)
    return jnp.clip(values, -bound, bound).astype(held_as)


def setup_inputs(seed: int = 0, part: int = 0) -> dict:
    arg_keys = jax.random.split(jax.random.key(seed), 9)
    part_splits = jax.random.split(jax.random.fold_in(arg_keys[8], part), 9)
    return {
        "out_grad": centred(part_splits[0], (SEQS, SEQ_LEN, D), 1.0, 6.0, ((0, 2), (1, 4), (2, 2))),
        "queries": draw_queries(jax.random.fold_in(jax.random.fold_in(arg_keys[8], part), 71), part),
        "keys": draw_keys(jax.random.fold_in(jax.random.fold_in(arg_keys[8], part), 71), part),
        "main_out": centred(part_splits[3], (SEQS, SPANS, D), 1.0, 6.0, ((0, 2), (1, 4), (2, 2))),
        "main_in_grad": centred(part_splits[4], (SEQS, SPANS, D), 1.0, 6.0, ((0, 2), (1, 4), (2, 2))),
        "boundaries": draw_boundaries(jax.random.fold_in(jax.random.fold_in(arg_keys[8], part), 71), part),
        "query_weight": centred(arg_keys[6], (D, D), D ** -0.5, 0.109375, ((0, 4), (1, 2))),
        "key_weight": centred(arg_keys[7], (D, D), D ** -0.5, 0.109375, ((0, 4), (1, 2))),
    }


epsilon = 1e-06

def reference(out_grad, queries, keys, main_out, main_in_grad, boundaries, query_weight, key_weight):
    block_width = D // N_TENSOR
    byte_list = []
    span_list = []
    for sequence in range(SEQS):
        cotangent = out_grad[sequence].astype(jnp.float32)
        query_wide = queries[sequence].astype(jnp.float32)
        key_rows = keys[sequence]
        bounds_row = boundaries[sequence]
        positions = jnp.arange(SEQ_LEN, dtype=jnp.int32)
        span_of = (jnp.searchsorted(bounds_row, positions, side='right') - 1).astype(jnp.int32)
        starts = jnp.take(bounds_row, span_of) == positions
        prev_keys = jnp.concatenate([jnp.zeros((1, D), jnp.bfloat16), key_rows[:-1]], 0)
        prev_wide = prev_keys.astype(jnp.float32)
        cross_sum = lax.optimization_barrier(jnp.sum(query_wide * prev_wide, 1))
        query_sum = lax.optimization_barrier(jnp.sum(query_wide * query_wide, 1))
        key_sum = lax.optimization_barrier(jnp.sum(prev_wide * prev_wide, 1))
        query_scale = lax.rsqrt(query_sum + epsilon)
        key_scale = lax.rsqrt(key_sum + epsilon)
        cosine = cross_sum * query_scale * key_scale
        probability = jnp.where(positions == 0, 1.0, 0.5 * (1.0 - cosine))
        confidence = jnp.where(starts, probability, 1.0 - probability)
        upsampled = jnp.take(main_out[sequence], span_of, axis=0).astype(jnp.float32)
        conf_grad = lax.optimization_barrier(jnp.sum(cotangent * upsampled, 1))
        span_sums = jax.ops.segment_sum(confidence[:, None] * cotangent, span_of, num_segments=SPANS)
        span_list.append(span_sums.astype(jnp.bfloat16))
        sign = jnp.where(starts, 1.0, -1.0)
        cos_grad = jnp.where(positions == 0, 0.0, -0.5 * sign * conf_grad)
        both_scale = (query_scale * key_scale)[:, None]
        query_grad = (cos_grad[:, None] * (prev_wide * both_scale - (cosine * query_scale * query_scale)[:, None] * query_wide)).astype(jnp.bfloat16)
        prev_grad = (cos_grad[:, None] * (query_wide * both_scale - (cosine * key_scale * key_scale)[:, None] * prev_wide)).astype(jnp.bfloat16)
        key_grad = jnp.concatenate([prev_grad[1:], jnp.zeros((1, D), jnp.bfloat16)], 0)
        routing = jnp.zeros((SEQ_LEN, D), jnp.float32)
        for block in range(N_TENSOR):
            first_col = block * block_width
            last_col = first_col + block_width
            partial_value = jnp.dot(query_grad[:, first_col:last_col], query_weight[:, first_col:last_col].T, preferred_element_type=jnp.float32)
            partial_value = partial_value + jnp.dot(key_grad[:, first_col:last_col], key_weight[:, first_col:last_col].T, preferred_element_type=jnp.float32)
            routing = routing + lax.optimization_barrier(partial_value.astype(jnp.bfloat16)).astype(jnp.float32)
        start_grad = jnp.where(starts[:, None], jnp.take(main_in_grad[sequence], span_of, axis=0).astype(jnp.float32), 0.0)
        byte_list.append((cotangent + start_grad + routing).astype(jnp.bfloat16))
    return (jnp.stack(byte_list), jnp.stack(span_list))
```

```python
import jax
import jax.numpy as jnp
from jax import lax
from jax.sharding import PartitionSpec as P

epsilon = 1e-06


def passed_along(x, axis, by):
    length = lax.axis_size(axis)
    pairs = [(i, i + by) for i in range(length) if 0 <= i + by < length]
    return lax.ppermute(x, axis, pairs)


def shards(out_grad, queries, keys, main_out, main_in_grad, boundaries, query_weight, key_weight):
    cotangent = out_grad[0]
    query_rows = queries[0]
    key_rows = keys[0]
    bounds_row = boundaries[0]
    row_count = cotangent.shape[0]
    span_rows = main_out.shape[1]
    shard_index = lax.axis_index("seq")
    seq_count = lax.axis_size("seq")
    positions = shard_index * row_count + jnp.arange(row_count, dtype=jnp.int32)
    span_of = jnp.sum((bounds_row[None, :] <= positions[:, None]).astype(jnp.int32), 1) - 1
    starts = jnp.any(bounds_row[None, :] == positions[:, None], 1)
    window_out, window_grad = (
        lax.all_gather(main_out[0], "seq", axis=0, tiled=True),
        lax.all_gather(main_in_grad[0], "seq", axis=0, tiled=True),
    )
    window_rows = window_out.shape[0]
    selector = span_of[:, None] == jnp.arange(window_rows, dtype=jnp.int32)[None, :]
    picker = selector.astype(jnp.bfloat16)
    upsampled = jnp.dot(picker, window_out, preferred_element_type=jnp.float32)
    start_picker = (selector & starts[:, None]).astype(jnp.bfloat16)
    start_grad = jnp.dot(start_picker, window_grad, preferred_element_type=jnp.float32)
    last_key = passed_along(key_rows[-1:], "seq", 1)
    prev_keys = jnp.concatenate([last_key, key_rows[:-1]], 0)
    query_wide = query_rows.astype(jnp.float32)
    prev_wide = prev_keys.astype(jnp.float32)
    cotangent_wide = cotangent.astype(jnp.float32)
    cross_part = jnp.sum(query_wide * prev_wide, 1)
    query_part = jnp.sum(query_wide * query_wide, 1)
    key_part = jnp.sum(prev_wide * prev_wide, 1)
    conf_part = jnp.sum(cotangent_wide * upsampled, 1)
    cross_sum, query_sum, key_sum = lax.psum((cross_part, query_part, key_part), "tensor")
    conf_grad = lax.psum(conf_part, "tensor")
    query_scale = lax.rsqrt(query_sum + epsilon)
    key_scale = lax.rsqrt(key_sum + epsilon)
    cosine = cross_sum * query_scale * key_scale
    probability = jnp.where(positions == 0, 1.0, 0.5 * (1.0 - cosine))
    confidence = jnp.where(starts, probability, 1.0 - probability)
    conf_high = confidence.astype(jnp.bfloat16)
    conf_low = (confidence - conf_high.astype(jnp.float32)).astype(jnp.bfloat16)
    zero_weight = jnp.zeros((), jnp.bfloat16)
    weight_high = jnp.where(selector, conf_high[:, None], zero_weight)
    weight_low = jnp.where(selector, conf_low[:, None], zero_weight)
    contract = (((0,), (0,)), ((), ()))
    span_terms = lax.dot_general(
        weight_high, cotangent, contract, preferred_element_type=jnp.float32
    )
    span_terms = span_terms + lax.dot_general(
        weight_low, cotangent, contract, preferred_element_type=jnp.float32
    )
    received = lax.all_to_all(
        span_terms.reshape(seq_count, span_rows, span_terms.shape[1]).astype(jnp.bfloat16),
        "seq",
        split_axis=0,
        concat_axis=0,
        tiled=True,
    ).astype(jnp.float32)
    span_sums = jnp.sum(received, 0)
    main_grad = span_sums.astype(jnp.bfloat16)[None]
    sign = jnp.where(starts, 1.0, -1.0)
    cos_grad = jnp.where(positions == 0, 0.0, -0.5 * sign * conf_grad)
    both_scale = (query_scale * key_scale)[:, None]
    query_grad = (
        cos_grad[:, None]
        * (prev_wide * both_scale - (cosine * query_scale * query_scale)[:, None] * query_wide)
    ).astype(jnp.bfloat16)
    prev_grad = (
        cos_grad[:, None]
        * (query_wide * both_scale - (cosine * key_scale * key_scale)[:, None] * prev_wide)
    ).astype(jnp.bfloat16)
    next_grad = passed_along(prev_grad[:1], "seq", -1)
    key_grad = jnp.concatenate([prev_grad[1:], next_grad], 0)
    part_rows = query_weight.shape[0] // (lax.axis_size("groups") * lax.axis_size("pipe"))
    part_index = lax.axis_index("groups") * lax.axis_size("pipe") + lax.axis_index("pipe")
    pieces = [
        lax.all_gather(
            lax.dynamic_slice_in_dim(weight, part_index * part_rows, part_rows, 0),
            ("seq", "groups", "pipe"),
            axis=0,
            tiled=True,
        )
        for weight in (query_weight, key_weight)
    ]
    partial_value = jnp.dot(query_grad, pieces[0].T, preferred_element_type=jnp.float32) + jnp.dot(
        key_grad, pieces[1].T, preferred_element_type=jnp.float32
    )
    routing = lax.psum_scatter(
        partial_value.astype(jnp.bfloat16), "tensor", scatter_dimension=1, tiled=True
    ).astype(jnp.float32)
    byte_grad = (cotangent_wide + start_grad + routing).astype(jnp.bfloat16)[None]
    return (byte_grad, main_grad)


def solution(mesh):
    return jax.shard_map(
        shards,
        mesh=mesh,
        in_specs=(
            P(("groups", "pipe"), "seq", "tensor"),
            P(("groups", "pipe"), "seq", "tensor"),
            P(("groups", "pipe"), "seq", "tensor"),
            P(("groups", "pipe"), "seq", "tensor"),
            P(("groups", "pipe"), "seq", "tensor"),
            P(("groups", "pipe"), None),
            P("seq", "tensor"),
            P("seq", "tensor"),
        ),
        out_specs=(P(("groups", "pipe"), "seq", "tensor"), P(("groups", "pipe"), "seq", "tensor")),
        check_vma=False,
    )
```

```python
import jax
import jax.numpy as jnp
from jax import lax
from jax.sharding import PartitionSpec as P

epsilon = 1e-06


def passed_along(x, axis, by):
    length = lax.axis_size(axis)
    pairs = [(i, i + by) for i in range(length) if 0 <= i + by < length]
    return lax.ppermute(x, axis, pairs)


reach = 2


def swapped(x, axis):
    length = lax.axis_size(axis)
    return lax.ppermute(x, axis, [(i, length - 1 - i) for i in range(length)])


def window_of(block):
    pieces = []
    for offset in range(-reach, reach + 1):
        pieces.append(block if offset == 0 else passed_along(block, "seq", -offset))
    return jnp.concatenate(pieces, 0)


def after(value, *others):
    return lax.optimization_barrier((value,) + others)[0]


def product(rows, weight):
    return lax.dot_general(
        rows, weight, (((1,), (1,)), ((), ())), preferred_element_type=jnp.float32
    )


def shards(out_grad, queries, keys, main_out, main_in_grad, boundaries, query_weight, key_weight):
    cotangent = out_grad[0]
    query_rows = queries[0]
    key_rows = keys[0]
    bounds_row = boundaries[0]
    row_count = cotangent.shape[0]
    span_rows = main_out.shape[1]
    shard_index = lax.axis_index("seq")
    seq_count = lax.axis_size("seq")
    tensor_count = lax.axis_size("tensor")
    tensor_index = lax.axis_index("tensor")
    group_index = lax.axis_index("groups")
    part_rows = query_weight.shape[0] // (lax.axis_size("groups") * lax.axis_size("pipe"))
    part_index = group_index * lax.axis_size("pipe") + lax.axis_index("pipe")
    query_part_weight, key_part_weight = [
        lax.all_gather(
            lax.dynamic_slice_in_dim(weight, part_index * part_rows, part_rows, 0),
            ("seq", "pipe"),
            axis=0,
            tiled=True,
        )
        for weight in (query_weight, key_weight)
    ]
    last_key = passed_along(key_rows[-1:], "seq", 1)
    window_out = window_of(main_out[0])
    positions = shard_index * row_count + jnp.arange(row_count, dtype=jnp.int32)
    span_of = jnp.sum((bounds_row[None, :] <= positions[:, None]).astype(jnp.int32), 1) - 1
    starts = jnp.any(bounds_row[None, :] == positions[:, None], 1)
    place = span_of - (shard_index - reach) * span_rows
    window_rows = window_out.shape[0]
    selector = place[:, None] == jnp.arange(window_rows, dtype=jnp.int32)[None, :]
    upsampled = jnp.dot(selector.astype(jnp.bfloat16), window_out, preferred_element_type=jnp.float32)
    prev_keys = jnp.concatenate([last_key, key_rows[:-1]], 0)
    query_wide = query_rows.astype(jnp.float32)
    prev_wide = prev_keys.astype(jnp.float32)
    cotangent_wide = cotangent.astype(jnp.float32)
    cross_part = jnp.sum(query_wide * prev_wide, 1)
    query_part = jnp.sum(query_wide * query_wide, 1)
    key_part = jnp.sum(prev_wide * prev_wide, 1)
    conf_part = jnp.sum(cotangent_wide * upsampled, 1)
    cross_sum, query_sum, key_sum, conf_grad = lax.psum(
        (cross_part, query_part, key_part, conf_part), "tensor"
    )
    query_scale = lax.rsqrt(query_sum + epsilon)
    key_scale = lax.rsqrt(key_sum + epsilon)
    cosine = cross_sum * query_scale * key_scale
    probability = jnp.where(positions == 0, 1.0, 0.5 * (1.0 - cosine))
    confidence = jnp.where(starts, probability, 1.0 - probability)
    sign = jnp.where(starts, 1.0, -1.0)
    cos_grad = jnp.where(positions == 0, 0.0, -0.5 * sign * conf_grad)
    both_scale = (query_scale * key_scale)[:, None]
    query_grad = (
        cos_grad[:, None]
        * (prev_wide * both_scale - (cosine * query_scale * query_scale)[:, None] * query_wide)
    ).astype(jnp.bfloat16)
    prev_grad = (
        cos_grad[:, None]
        * (query_wide * both_scale - (cosine * key_scale * key_scale)[:, None] * prev_wide)
    ).astype(jnp.bfloat16)
    next_grad = passed_along(prev_grad[:1], "seq", -1)
    query_grad_other = swapped(query_grad, "groups")
    key_grad = jnp.concatenate([prev_grad[1:], next_grad], 0)
    key_grad_other = swapped(key_grad, "groups")

    conf_high = confidence.astype(jnp.bfloat16)
    conf_low = (confidence - conf_high.astype(jnp.float32)).astype(jnp.bfloat16)
    zero_weight = jnp.zeros((), jnp.bfloat16)
    weight_high = jnp.where(selector, conf_high[:, None], zero_weight)
    weight_low = jnp.where(selector, conf_low[:, None], zero_weight)
    contract = (((0,), (0,)), ((), ()))
    span_terms = lax.dot_general(
        weight_high, cotangent, contract, preferred_element_type=jnp.float32
    )
    span_terms = span_terms + lax.dot_general(
        weight_low, cotangent, contract, preferred_element_type=jnp.float32
    )
    grad_block = after(main_in_grad[0], query_part_weight)
    window_grad = window_of(grad_block)
    start_picker = (selector & starts[:, None]).astype(jnp.bfloat16)
    start_grad = jnp.dot(start_picker, window_grad, preferred_element_type=jnp.float32)
    span_sums = span_terms[reach * span_rows : (reach + 1) * span_rows]
    for offset in range(-reach, reach + 1):
        if offset != 0:
            block = span_terms[(reach + offset) * span_rows : (reach + offset + 1) * span_rows]
            block = block.astype(jnp.bfloat16)
            span_sums = span_sums + passed_along(block, "seq", offset).astype(jnp.float32)
    main_grad = span_sums.astype(jnp.bfloat16)[None]

    def partial(query_side, key_side, query_block, key_block):
        total = product(query_side, query_block) + product(key_side, key_block)
        return total.astype(jnp.bfloat16)

    block_rows = query_part_weight.shape[0] // tensor_count
    if tensor_count == 2:

        def half(weight, index):
            return lax.dynamic_slice_in_dim(weight, index * block_rows, block_rows, 0)

        query_far, key_far = half(query_part_weight, 1 - tensor_index), half(key_part_weight, 1 - tensor_index)
        query_near, key_near = half(query_part_weight, tensor_index), half(key_part_weight, tensor_index)
        other_in = swapped(partial(query_grad_other, key_grad_other, query_far, key_far), "tensor")
        own_in = swapped(partial(query_grad, key_grad, query_far, key_far), "tensor")
        other_near = partial(query_grad_other, key_grad_other, query_near, key_near)
        own_near = partial(query_grad, key_grad, query_near, key_near)
        other_sum = other_near.astype(jnp.float32) + other_in.astype(jnp.float32)
        own_sum = own_near.astype(jnp.float32) + own_in.astype(jnp.float32)
    else:
        other_sum = lax.psum_scatter(
            partial(query_grad_other, key_grad_other, query_part_weight, key_part_weight),
            "tensor",
            scatter_dimension=1,
            tiled=True,
        )
        own_sum = lax.psum_scatter(
            partial(query_grad, key_grad, query_part_weight, key_part_weight),
            "tensor",
            scatter_dimension=1,
            tiled=True,
        ).astype(jnp.float32)
    from_other = swapped(other_sum.astype(jnp.bfloat16), "groups").astype(jnp.float32)
    first = jnp.where(group_index == 0, own_sum, from_other)
    second = jnp.where(group_index == 0, from_other, own_sum)
    width = part_rows * lax.axis_size("pipe")
    columns = []
    for start in range(0, block_rows, width):
        columns += [first[:, start : start + width], second[:, start : start + width]]
    routing = jnp.concatenate(columns, 1)
    byte_grad = (cotangent_wide + start_grad + routing).astype(jnp.bfloat16)[None]
    return (byte_grad, main_grad)


def solution(mesh):
    return jax.shard_map(
        shards,
        mesh=mesh,
        in_specs=(
            P(("groups", "pipe"), "seq", "tensor"),
            P(("groups", "pipe"), "seq", "tensor"),
            P(("groups", "pipe"), "seq", "tensor"),
            P(("groups", "pipe"), "seq", "tensor"),
            P(("groups", "pipe"), "seq", "tensor"),
            P(("groups", "pipe"), None),
            P("seq", "tensor"),
            P("seq", "tensor"),
        ),
        out_specs=(P(("groups", "pipe"), "seq", "tensor"), P(("groups", "pipe"), "seq", "tensor")),
        check_vma=False,
    )
```

```python
import jax
import jax.numpy as jnp
from jax import lax
from jax.sharding import PartitionSpec as P

epsilon = 1e-06


def passed_along(x, axis, by):
    length = lax.axis_size(axis)
    pairs = [(i, i + by) for i in range(length) if 0 <= i + by < length]
    return lax.ppermute(x, axis, pairs)


reach = 2


def swapped(x, axis):
    length = lax.axis_size(axis)
    return lax.ppermute(x, axis, [(i, length - 1 - i) for i in range(length)])


def passed_across(x, by):
    group_count, length = lax.axis_size("groups"), lax.axis_size("seq")
    pairs = [
        (g * length + i, (group_count - 1 - g) * length + i + by)
        for g in range(group_count)
        for i in range(length)
        if 0 <= i + by < length
    ]
    return lax.ppermute(x, ("groups", "seq"), pairs)


def window_of(block):
    right = passed_along(block, "seq", 1)
    left = passed_along(block, "seq", -1)
    far_right = passed_along(right, "seq", 1)
    far_left = passed_along(left, "seq", -1)
    return jnp.concatenate([far_right, right, block, left, far_left], 0)


def after(value, *others):
    return lax.optimization_barrier((value,) + others)[0]


def product(rows, weight):
    return lax.dot_general(
        rows, weight, (((1,), (1,)), ((), ())), preferred_element_type=jnp.float32
    )


def shards(out_grad, queries, keys, main_out, main_in_grad, boundaries, query_weight, key_weight):
    cotangent = out_grad[0]
    query_rows = queries[0]
    key_rows = keys[0]
    bounds_row = boundaries[0]
    row_count = cotangent.shape[0]
    span_rows = main_out.shape[1]
    shard_index = lax.axis_index("seq")
    seq_count = lax.axis_size("seq")
    tensor_count = lax.axis_size("tensor")
    tensor_index = lax.axis_index("tensor")
    group_index = lax.axis_index("groups")
    pipe_index = lax.axis_index("pipe")
    group_rows = query_weight.shape[0] // lax.axis_size("groups")
    half_cols = query_weight.shape[1] // lax.axis_size("pipe")

    def columns(x, index):
        return lax.dynamic_slice_in_dim(x, index * half_cols, half_cols, 1)

    first_rows = group_rows * 2 // 3 // 16 * 16
    cuts = [(0, first_rows), (first_rows, group_rows)]
    own_weights = []
    for low, high in cuts:
        piece = jnp.concatenate(
            [
                lax.dynamic_slice(
                    weight,
                    (group_index * group_rows + low, pipe_index * half_cols),
                    (high - low, half_cols),
                )
                for weight in (query_weight, key_weight)
            ],
            1,
        )
        own_weights.append(lax.all_gather(piece, "seq", axis=0, tiled=True))
    window_out = window_of(main_out[0])
    last_key = passed_along(key_rows[-1:], "seq", 1)
    next_query = passed_along(query_rows[:1], "seq", -1)
    query_other = swapped(query_rows, "groups")
    key_other = swapped(key_rows, "groups")
    last_key_other = passed_across(key_rows[-1:], 1)
    next_query_other = passed_across(query_rows[:1], -1)
    other_weights = [swapped(weight, "pipe") for weight in own_weights]

    positions = shard_index * row_count + jnp.arange(row_count, dtype=jnp.int32)
    span_of = jnp.sum((bounds_row[None, :] <= positions[:, None]).astype(jnp.int32), 1) - 1
    starts = jnp.any(bounds_row[None, :] == positions[:, None], 1)
    place = span_of - (shard_index - reach) * span_rows
    window_rows = window_out.shape[0]
    selector = place[:, None] == jnp.arange(window_rows, dtype=jnp.int32)[None, :]
    upsampled = jnp.dot(selector.astype(jnp.bfloat16), window_out, preferred_element_type=jnp.float32)
    prev_keys = jnp.concatenate([last_key, key_rows[:-1]], 0)
    query_wide = query_rows.astype(jnp.float32)
    prev_wide = prev_keys.astype(jnp.float32)
    cotangent_wide = cotangent.astype(jnp.float32)
    sums = jnp.stack(
        [
            jnp.sum(query_wide * prev_wide, 1),
            jnp.sum(query_wide * query_wide, 1),
            jnp.sum(prev_wide * prev_wide, 1),
            jnp.sum(cotangent_wide * upsampled, 1),
        ]
    )
    if tensor_count == 2:
        sums = sums + swapped(sums, "tensor")
    else:
        sums = lax.psum(sums, "tensor")
    cross_sum, query_sum, key_sum, conf_grad = sums
    query_scale = lax.rsqrt(query_sum + epsilon)
    key_scale = lax.rsqrt(key_sum + epsilon)
    cosine = cross_sum * query_scale * key_scale
    probability = jnp.where(positions == 0, 1.0, 0.5 * (1.0 - cosine))
    confidence = jnp.where(starts, probability, 1.0 - probability)
    sign = jnp.where(starts, 1.0, -1.0)
    cos_grad = jnp.where(positions == 0, 0.0, -0.5 * sign * conf_grad)
    factors = jnp.stack(
        [
            cos_grad * (query_scale * key_scale),
            cos_grad * (cosine * query_scale * query_scale),
            cos_grad * (cosine * key_scale * key_scale),
        ]
    )
    next_factors = passed_along(factors[:, :1], "seq", -1)
    factors_other = swapped(factors, "groups")
    next_factors_other = passed_across(factors[:, :1], -1)

    def grads(queries_here, keys_here, key_before, query_after, here, after_here, index):
        previous = jnp.concatenate([columns(key_before, index), columns(keys_here, index)[:-1]], 0)
        current = columns(queries_here, index)
        following = jnp.concatenate([current[1:], columns(query_after, index)], 0)
        ahead = jnp.concatenate([here[:, 1:], after_here], 1)
        query_grad = here[0][:, None] * previous.astype(jnp.float32)
        query_grad = query_grad - here[1][:, None] * current.astype(jnp.float32)
        key_grad = ahead[0][:, None] * following.astype(jnp.float32)
        key_grad = key_grad - ahead[2][:, None] * columns(keys_here, index).astype(jnp.float32)
        return jnp.concatenate([query_grad.astype(jnp.bfloat16), key_grad.astype(jnp.bfloat16)], 1)

    def both_grads(index):
        own = grads(query_rows, key_rows, last_key, next_query, factors, next_factors, index)
        other = grads(
            query_other,
            key_other,
            last_key_other,
            next_query_other,
            factors_other,
            next_factors_other,
            index,
        )
        return jnp.concatenate([own, other], 0)

    own_side, other_side = both_grads(pipe_index), both_grads(1 - pipe_index)

    conf_high = confidence.astype(jnp.bfloat16)
    conf_low = (confidence - conf_high.astype(jnp.float32)).astype(jnp.bfloat16)
    zero_weight = jnp.zeros((), jnp.bfloat16)
    weight_high = jnp.where(selector, conf_high[:, None], zero_weight)
    weight_low = jnp.where(selector, conf_low[:, None], zero_weight)
    contract = (((0,), (0,)), ((), ()))
    span_terms = lax.dot_general(
        weight_high, cotangent, contract, preferred_element_type=jnp.float32
    )
    span_terms = span_terms + lax.dot_general(
        weight_low, cotangent, contract, preferred_element_type=jnp.float32
    )
    terms = [span_terms[i * span_rows : (i + 1) * span_rows] for i in range(2 * reach + 1)]

    def moved(block, by):
        return passed_along(block.astype(jnp.bfloat16), "seq", by).astype(jnp.float32)

    span_sums = terms[2] + moved(terms[3] + moved(terms[4], 1), 1) + moved(terms[1] + moved(terms[0], -1), -1)
    main_grad = span_sums.astype(jnp.bfloat16)[None]
    grad_block = after(main_in_grad[0], own_weights[0])
    window_grad = window_of(grad_block)
    start_picker = (selector & starts[:, None]).astype(jnp.bfloat16)
    start_grad = jnp.dot(start_picker, window_grad, preferred_element_type=jnp.float32)

    def partial(own_weight, other_weight):
        total = product(own_side, own_weight) + product(other_side, other_weight)
        return total.astype(jnp.bfloat16)

    pieces = []
    for own_weight, other_weight in zip(own_weights, other_weights):
        block_rows = own_weight.shape[0] // tensor_count
        if tensor_count == 2:

            def half(index):
                return [
                    lax.dynamic_slice_in_dim(weight, index * block_rows, block_rows, 0)
                    for weight in (own_weight, other_weight)
                ]

            incoming = swapped(partial(*half(1 - tensor_index)), "tensor").astype(jnp.float32)
            total = partial(*half(tensor_index)).astype(jnp.float32) + incoming
        else:
            total = lax.psum_scatter(
                partial(own_weight, other_weight), "tensor", scatter_dimension=1, tiled=True
            ).astype(jnp.float32)
        own = total[:row_count]
        arrived = swapped(total[row_count:].astype(jnp.bfloat16), "groups").astype(jnp.float32)
        pieces.append(
            [jnp.where(group_index == 0, own, arrived), jnp.where(group_index == 0, arrived, own)]
        )
    widths = [high - low for low, high in cuts]
    routing = jnp.concatenate(
        [
            piece[group][:, s * width : (s + 1) * width]
            for s in range(seq_count // tensor_count)
            for group in range(2)
            for piece, width in zip(pieces, widths)
        ],
        1,
    )
    byte_grad = (cotangent_wide + start_grad + routing).astype(jnp.bfloat16)[None]
    return (byte_grad, main_grad)


def solution(mesh):
    return jax.shard_map(
        shards,
        mesh=mesh,
        in_specs=(
            P(("groups", "pipe"), "seq", "tensor"),
            P(("groups", "pipe"), "seq", "tensor"),
            P(("groups", "pipe"), "seq", "tensor"),
            P(("groups", "pipe"), "seq", "tensor"),
            P(("groups", "pipe"), "seq", "tensor"),
            P(("groups", "pipe"), None),
            P("seq", "tensor"),
            P("seq", "tensor"),
        ),
        out_specs=(P(("groups", "pipe"), "seq", "tensor"), P(("groups", "pipe"), "seq", "tensor")),
        check_vma=False,
    )
```

```python
import jax
import jax.numpy as jnp
from jax import lax
from jax.experimental import pallas as pl
from jax.sharding import PartitionSpec as P

epsilon = 1e-06


def passed_along(x, axis, by):
    length = lax.axis_size(axis)
    pairs = [(i, i + by) for i in range(length) if 0 <= i + by < length]
    return lax.ppermute(x, axis, pairs)


reach = 2


def swapped(x, axis):
    length = lax.axis_size(axis)
    return lax.ppermute(x, axis, [(i, length - 1 - i) for i in range(length)])


def passed_across(x, by):
    group_count, length = lax.axis_size("groups"), lax.axis_size("seq")
    pairs = [
        (g * length + i, (group_count - 1 - g) * length + i + by)
        for g in range(group_count)
        for i in range(length)
        if 0 <= i + by < length
    ]
    return lax.ppermute(x, ("groups", "seq"), pairs)


def passed_on(x, axis, by, came_from):
    length = lax.axis_size(axis)
    pairs = [
        (i, i + by) for i in range(length) if 0 <= i + by < length and 0 <= i + came_from < length
    ]
    return lax.ppermute(x, axis, pairs)


def neighbours(block):
    return passed_along(block, "seq", 1), passed_along(block, "seq", -1)


def second_neighbours(right, left):
    return passed_on(right, "seq", 1, -1), passed_on(left, "seq", -1, 1)


def after(value, *others):
    def kernel(*refs):
        del refs

    anywhere = pl.BlockSpec(memory_space=pl.ANY)
    return pl.pallas_call(
        kernel,
        out_shape=jax.ShapeDtypeStruct(value.shape, value.dtype),
        in_specs=[anywhere] * (1 + len(others)),
        out_specs=anywhere,
        input_output_aliases={0: 0},
        name="after",
    )(value, *others)


def product(rows, weight):
    return lax.dot_general(
        rows, weight, (((1,), (1,)), ((), ())), preferred_element_type=jnp.float32
    )


def shards(out_grad, queries, keys, main_out, main_in_grad, boundaries, query_weight, key_weight):
    cotangent = out_grad[0]
    query_rows = queries[0]
    key_rows = keys[0]
    bounds_row = boundaries[0]
    row_count = cotangent.shape[0]
    span_rows = main_out.shape[1]
    shard_index = lax.axis_index("seq")
    seq_count = lax.axis_size("seq")
    tensor_count = lax.axis_size("tensor")
    tensor_index = lax.axis_index("tensor")
    group_index = lax.axis_index("groups")
    pipe_index = lax.axis_index("pipe")
    group_rows = query_weight.shape[0] // lax.axis_size("groups")
    half_cols = query_weight.shape[1] // lax.axis_size("pipe")

    def columns(x, index):
        return lax.dynamic_slice_in_dim(x, index * half_cols, half_cols, 1)

    first_rows = group_rows * 2 // 3 // 16 * 16
    cuts = [(0, first_rows), (first_rows, group_rows)]
    out_right, out_left = neighbours(main_out[0])
    query_other = swapped(query_rows, "groups")
    key_other = swapped(key_rows, "groups")
    own_weights = []
    for low, high in cuts:
        piece = jnp.concatenate(
            [
                lax.dynamic_slice(
                    weight,
                    (group_index * group_rows + low, pipe_index * half_cols),
                    (high - low, half_cols),
                )
                for weight in (query_weight, key_weight)
            ],
            1,
        )
        if own_weights:
            piece = after(piece, out_right)
        own_weights.append(lax.all_gather(piece, "seq", axis=0, tiled=True))
    out_far_right, out_far_left = second_neighbours(out_right, out_left)
    out_far_left = after(out_far_left, query_other, key_other)
    window_out = jnp.concatenate(
        [out_far_right, out_right, main_out[0], out_left, out_far_left], 0
    )
    last_key = passed_along(key_rows[-1:], "seq", 1)
    next_query = passed_along(query_rows[:1], "seq", -1)
    last_key_other = passed_across(key_rows[-1:], 1)
    next_query_other = passed_across(query_rows[:1], -1)

    positions = shard_index * row_count + jnp.arange(row_count, dtype=jnp.int32)
    span_of = jnp.sum((bounds_row[None, :] <= positions[:, None]).astype(jnp.int32), 1) - 1
    starts = jnp.any(bounds_row[None, :] == positions[:, None], 1)
    place = span_of - (shard_index - reach) * span_rows
    window_rows = window_out.shape[0]
    selector = place[:, None] == jnp.arange(window_rows, dtype=jnp.int32)[None, :]
    upsampled = jnp.dot(selector.astype(jnp.bfloat16), window_out, preferred_element_type=jnp.float32)
    prev_keys = jnp.concatenate([last_key, key_rows[:-1]], 0)
    query_wide = query_rows.astype(jnp.float32)
    prev_wide = prev_keys.astype(jnp.float32)
    cotangent_wide = cotangent.astype(jnp.float32)
    sums = jnp.stack(
        [
            jnp.sum(query_wide * prev_wide, 1),
            jnp.sum(query_wide * query_wide, 1),
            jnp.sum(prev_wide * prev_wide, 1),
            jnp.sum(cotangent_wide * upsampled, 1),
        ]
    )
    if tensor_count == 2:
        sums = sums + swapped(sums, "tensor")
    else:
        sums = lax.psum(sums, "tensor")
    cross_sum, query_sum, key_sum, conf_grad = sums
    query_scale = lax.rsqrt(query_sum + epsilon)
    key_scale = lax.rsqrt(key_sum + epsilon)
    cosine = cross_sum * query_scale * key_scale
    probability = jnp.where(positions == 0, 1.0, 0.5 * (1.0 - cosine))
    confidence = jnp.where(starts, probability, 1.0 - probability)
    sign = jnp.where(starts, 1.0, -1.0)
    cos_grad = jnp.where(positions == 0, 0.0, -0.5 * sign * conf_grad)
    factors = jnp.stack(
        [
            cos_grad * (query_scale * key_scale),
            cos_grad * (cosine * query_scale * query_scale),
            cos_grad * (cosine * key_scale * key_scale),
        ]
    )
    next_factors = passed_along(factors[:, :1], "seq", -1)
    factors_other = swapped(factors, "groups")
    next_factors_other = passed_across(factors[:, :1], -1)

    def grads(queries_here, keys_here, key_before, query_after, here, after_here, index):
        previous = jnp.concatenate([columns(key_before, index), columns(keys_here, index)[:-1]], 0)
        current = columns(queries_here, index)
        following = jnp.concatenate([current[1:], columns(query_after, index)], 0)
        ahead = jnp.concatenate([here[:, 1:], after_here], 1)
        query_grad = here[0][:, None] * previous.astype(jnp.float32)
        query_grad = query_grad - here[1][:, None] * current.astype(jnp.float32)
        key_grad = ahead[0][:, None] * following.astype(jnp.float32)
        key_grad = key_grad - ahead[2][:, None] * columns(keys_here, index).astype(jnp.float32)
        return jnp.concatenate([query_grad.astype(jnp.bfloat16), key_grad.astype(jnp.bfloat16)], 1)

    def both_grads(index):
        own = grads(query_rows, key_rows, last_key, next_query, factors, next_factors, index)
        other = grads(
            query_other,
            key_other,
            last_key_other,
            next_query_other,
            factors_other,
            next_factors_other,
            index,
        )
        return jnp.concatenate([own, other], 0)

    own_side, other_side = both_grads(pipe_index), both_grads(1 - pipe_index)

    conf_high = confidence.astype(jnp.bfloat16)
    conf_low = (confidence - conf_high.astype(jnp.float32)).astype(jnp.bfloat16)
    zero_weight = jnp.zeros((), jnp.bfloat16)
    weight_high = jnp.where(selector, conf_high[:, None], zero_weight)
    weight_low = jnp.where(selector, conf_low[:, None], zero_weight)
    contract = (((0,), (0,)), ((), ()))
    span_terms = lax.dot_general(
        weight_high, cotangent, contract, preferred_element_type=jnp.float32
    )
    span_terms = span_terms + lax.dot_general(
        weight_low, cotangent, contract, preferred_element_type=jnp.float32
    )
    terms = [span_terms[i * span_rows : (i + 1) * span_rows] for i in range(2 * reach + 1)]

    def moved(block, by, further):
        moved_block = passed_on(block.astype(jnp.bfloat16), "seq", by, further)
        return moved_block.astype(jnp.float32)

    span_sums = terms[2] + moved(terms[3] + moved(terms[4], 1, 2), 1, 1)
    span_sums = span_sums + moved(terms[1] + moved(terms[0], -1, -2), -1, -1)
    main_grad = span_sums.astype(jnp.bfloat16)[None]
    grad_right, grad_left = neighbours(after(main_in_grad[0], own_weights[0]))
    grad_far_right, grad_far_left = second_neighbours(grad_right, grad_left)
    window_grad = jnp.concatenate(
        [grad_far_right, grad_right, main_in_grad[0], grad_left, grad_far_left], 0
    )
    start_picker = (selector & starts[:, None]).astype(jnp.bfloat16)
    start_grad = jnp.dot(start_picker, window_grad, preferred_element_type=jnp.float32)

    def partial(own_weight, other_weight):
        total = product(own_side, own_weight) + product(other_side, other_weight)
        return total.astype(jnp.bfloat16)

    pieces = []
    far_part = None
    for own_weight in own_weights:
        if far_part is not None:
            own_weight = after(own_weight, far_part)
        other_weight = swapped(own_weight, "pipe")
        block_rows = own_weight.shape[0] // tensor_count
        if tensor_count == 2:

            def half(index):
                return [
                    lax.dynamic_slice_in_dim(weight, index * block_rows, block_rows, 0)
                    for weight in (own_weight, other_weight)
                ]

            far_part = partial(*half(1 - tensor_index))
            incoming = swapped(far_part, "tensor").astype(jnp.float32)
            total = partial(*half(tensor_index)).astype(jnp.float32) + incoming
        else:
            total = lax.psum_scatter(
                partial(own_weight, other_weight), "tensor", scatter_dimension=1, tiled=True
            ).astype(jnp.float32)
        own = total[:row_count]
        returned = total[row_count:].astype(jnp.bfloat16)
        if not pieces:
            returned = after(returned, grad_right, grad_left)
        arrived = swapped(returned, "groups").astype(jnp.float32)
        pieces.append(
            [jnp.where(group_index == 0, own, arrived), jnp.where(group_index == 0, arrived, own)]
        )
    widths = [high - low for low, high in cuts]
    routing = jnp.concatenate(
        [
            piece[group][:, s * width : (s + 1) * width]
            for s in range(seq_count // tensor_count)
            for group in range(2)
            for piece, width in zip(pieces, widths)
        ],
        1,
    )
    byte_grad = (cotangent_wide + start_grad + routing).astype(jnp.bfloat16)[None]
    return (byte_grad, main_grad)


def solution(mesh):
    return jax.shard_map(
        shards,
        mesh=mesh,
        in_specs=(
            P(("groups", "pipe"), "seq", "tensor"),
            P(("groups", "pipe"), "seq", "tensor"),
            P(("groups", "pipe"), "seq", "tensor"),
            P(("groups", "pipe"), "seq", "tensor"),
            P(("groups", "pipe"), "seq", "tensor"),
            P(("groups", "pipe"), None),
            P("seq", "tensor"),
            P("seq", "tensor"),
        ),
        out_specs=(P(("groups", "pipe"), "seq", "tensor"), P(("groups", "pipe"), "seq", "tensor")),
        check_vma=False,
    )
```

```python
import jax
import jax.numpy as jnp
from jax import lax
from jax.experimental import pallas as pl
from jax.experimental.pallas import tpu as pltpu
from jax.sharding import PartitionSpec as P

epsilon = 1e-06


def passed_along(x, axis, by):
    length = lax.axis_size(axis)
    pairs = [(i, i + by) for i in range(length) if 0 <= i + by < length]
    return lax.ppermute(x, axis, pairs)


reach = 2


def swapped(x, axis):
    length = lax.axis_size(axis)
    return lax.ppermute(x, axis, [(i, length - 1 - i) for i in range(length)])


def passed_on(x, axis, by, came_from):
    length = lax.axis_size(axis)
    pairs = [
        (i, i + by) for i in range(length) if 0 <= i + by < length and 0 <= i + came_from < length
    ]
    return lax.ppermute(x, axis, pairs)


def second_neighbours(right, left):
    return passed_on(right, "seq", 1, -1), passed_on(left, "seq", -1, 1)


def after(value, *others):
    def kernel(*refs):
        del refs

    anywhere = pl.BlockSpec(memory_space=pl.ANY)
    return pl.pallas_call(
        kernel,
        out_shape=jax.ShapeDtypeStruct(value.shape, value.dtype),
        in_specs=[anywhere] * (1 + len(others)),
        out_specs=anywhere,
        input_output_aliases={0: 0},
        name="after",
    )(value, *others)


def byte_sums_kernel(shard_ref, bounds_ref, cotangent_ref, query_ref, key_ref, *refs):
    blocks, out_ref = refs[:-1], refs[-1]
    rows, width = query_ref.shape
    span_rows = blocks[reach].shape[0]
    shard = shard_ref[0]
    row = lax.broadcasted_iota(jnp.int32, (rows, 1), 0)
    held = (bounds_ref[...] <= shard * rows + row).astype(jnp.float32)
    span_of = jnp.sum(held, 1, keepdims=True).astype(jnp.int32) - 1
    place = span_of - (shard - reach) * span_rows
    column = lax.broadcasted_iota(jnp.int32, (rows, span_rows), 1)
    pickers = [
        (place - i * span_rows == column).astype(jnp.float32).astype(jnp.bfloat16)
        for i in range(len(blocks))
    ]
    last_row = blocks[reach - 1].shape[0] - 1
    tile = 384
    totals = [jnp.zeros((rows, 128), jnp.float32)] * 4
    for start in range(0, width, tile):
        cols = pl.ds(start, tile)
        upsampled = jnp.zeros((rows, tile), jnp.float32)
        for picker, block in zip(pickers, blocks):
            upsampled = upsampled + jnp.dot(
                picker, block[:span_rows, cols], preferred_element_type=jnp.float32
            )
        query = query_ref[:, cols].astype(jnp.float32)
        previous = pltpu.roll(key_ref[:, cols].astype(jnp.float32), 1, 0)
        edge = blocks[reach - 1][last_row - 15 :, cols].astype(jnp.float32)[15:16]
        previous = jnp.where(row == 0, edge, previous)
        cotangent = cotangent_ref[:, cols].astype(jnp.float32)
        terms = [query * previous, query * query, previous * previous, cotangent * upsampled]
        for piece in range(0, tile, 128):
            totals = [
                total + term[:, piece : piece + 128] for total, term in zip(totals, terms)
            ]
    lines = [jnp.sum(total.T, 0, keepdims=True) for total in totals]
    out_ref[...] = jnp.concatenate(lines + [jnp.zeros((4, rows), jnp.float32)], 0)


def byte_sums(shard_index, bounds, cotangent, query_rows, key_rows, blocks):
    rows = query_rows.shape[0]
    vmem = pl.BlockSpec(memory_space=pltpu.VMEM)
    return pl.pallas_call(
        byte_sums_kernel,
        out_shape=jax.ShapeDtypeStruct((8, rows), jnp.float32),
        in_specs=[pl.BlockSpec(memory_space=pltpu.SMEM)] + [vmem] * (4 + len(blocks)),
        out_specs=vmem,
        compiler_params=pltpu.CompilerParams(vmem_limit_bytes=40 * 1024 * 1024),
        name="byte_sums",
    )(shard_index[None], bounds, cotangent, query_rows, key_rows, *blocks)


def product(rows, weight):
    return lax.dot_general(
        rows, weight, (((1,), (1,)), ((), ())), preferred_element_type=jnp.float32
    )


def shards(out_grad, queries, keys, main_out, main_in_grad, boundaries, query_weight, key_weight):
    cotangent = out_grad[0]
    query_rows = queries[0]
    key_rows = keys[0]
    bounds_row = boundaries[0]
    row_count = cotangent.shape[0]
    span_rows = main_out.shape[1]
    shard_index = lax.axis_index("seq")
    seq_count = lax.axis_size("seq")
    tensor_count = lax.axis_size("tensor")
    tensor_index = lax.axis_index("tensor")
    group_index = lax.axis_index("groups")
    pipe_index = lax.axis_index("pipe")
    group_rows = query_weight.shape[0] // lax.axis_size("groups")
    half_cols = query_weight.shape[1] // lax.axis_size("pipe")

    def columns(x, index):
        return lax.dynamic_slice_in_dim(x, index * half_cols, half_cols, 1)

    first_rows = group_rows * 2 // 3 // 16 * 16
    cuts = [(0, first_rows), (first_rows, group_rows)]
    out_right = passed_along(jnp.concatenate([main_out[0], key_rows[-16:]], 0), "seq", 1)
    out_left = passed_along(jnp.concatenate([main_out[0], query_rows[:16]], 0), "seq", -1)
    query_other = swapped(query_rows, "groups")
    key_other = swapped(key_rows, "groups")
    own_weights = []
    for low, high in cuts:
        piece = jnp.concatenate(
            [
                lax.dynamic_slice(
                    weight,
                    (group_index * group_rows + low, pipe_index * half_cols),
                    (high - low, half_cols),
                )
                for weight in (query_weight, key_weight)
            ],
            1,
        )
        if own_weights:
            piece = after(piece, out_right)
        own_weights.append(lax.all_gather(piece, "seq", axis=0, tiled=True))
    out_far_right, out_far_left = second_neighbours(out_right, out_left)
    last_key, next_query = out_right[-1:], out_left[span_rows : span_rows + 1]
    edges_other = swapped(jnp.concatenate([last_key, next_query], 0), "groups")
    last_key_other, next_query_other = edges_other[:1], edges_other[1:]
    blocks = [out_far_right, out_right, main_out[0], out_left, out_far_left]
    sums = byte_sums(shard_index, boundaries, cotangent, query_rows, key_rows, blocks)

    positions = shard_index * row_count + jnp.arange(row_count, dtype=jnp.int32)
    span_of = jnp.sum((bounds_row[None, :] <= positions[:, None]).astype(jnp.int32), 1) - 1
    starts = jnp.any(bounds_row[None, :] == positions[:, None], 1)
    place = span_of - (shard_index - reach) * span_rows
    window_rows = (2 * reach + 1) * span_rows
    selector = place[:, None] == jnp.arange(window_rows, dtype=jnp.int32)[None, :]
    cotangent_wide = cotangent.astype(jnp.float32)
    if tensor_count == 2:
        sums = sums + swapped(sums, "tensor")
    else:
        sums = lax.psum(sums, "tensor")
    cross_sum, query_sum, key_sum, conf_grad = sums[:4]
    query_scale = lax.rsqrt(query_sum + epsilon)
    key_scale = lax.rsqrt(key_sum + epsilon)
    cosine = cross_sum * query_scale * key_scale
    probability = jnp.where(positions == 0, 1.0, 0.5 * (1.0 - cosine))
    confidence = jnp.where(starts, probability, 1.0 - probability)
    sign = jnp.where(starts, 1.0, -1.0)
    cos_grad = jnp.where(positions == 0, 0.0, -0.5 * sign * conf_grad)
    factors = jnp.stack(
        [
            cos_grad * (query_scale * key_scale),
            cos_grad * (cosine * query_scale * query_scale),
            cos_grad * (cosine * key_scale * key_scale),
        ]
    )
    next_factors = passed_along(factors[:, :1], "seq", -1)
    factors = jnp.concatenate([factors, next_factors], 1)
    factors_other = swapped(factors, "groups")

    def grads(queries_here, keys_here, key_before, query_after, here, index):
        previous = jnp.concatenate([columns(key_before, index), columns(keys_here, index)[:-1]], 0)
        current = columns(queries_here, index)
        following = jnp.concatenate([current[1:], columns(query_after, index)], 0)
        ahead, here = here[:, 1:], here[:, :-1]
        query_grad = here[0][:, None] * previous.astype(jnp.float32)
        query_grad = query_grad - here[1][:, None] * current.astype(jnp.float32)
        key_grad = ahead[0][:, None] * following.astype(jnp.float32)
        key_grad = key_grad - ahead[2][:, None] * columns(keys_here, index).astype(jnp.float32)
        return jnp.concatenate([query_grad.astype(jnp.bfloat16), key_grad.astype(jnp.bfloat16)], 1)

    def both_grads(index):
        own = grads(query_rows, key_rows, last_key, next_query, factors, index)
        other = grads(
            query_other,
            key_other,
            last_key_other,
            next_query_other,
            factors_other,
            index,
        )
        return jnp.concatenate([own, other], 0)

    own_side, other_side = both_grads(pipe_index), both_grads(1 - pipe_index)

    def span_part(ready):
        conf_high = confidence.astype(jnp.bfloat16)
        conf_low = (confidence - conf_high.astype(jnp.float32)).astype(jnp.bfloat16)
        zero_weight = jnp.zeros((), jnp.bfloat16)
        weight_high = jnp.where(selector, conf_high[:, None], zero_weight)
        weight_low = jnp.where(selector, conf_low[:, None], zero_weight)
        contract = (((0,), (0,)), ((), ()))
        span_terms = lax.dot_general(
            weight_high, cotangent, contract, preferred_element_type=jnp.float32
        )
        span_terms = span_terms + lax.dot_general(
            weight_low, cotangent, contract, preferred_element_type=jnp.float32
        )
        terms = [span_terms[i * span_rows : (i + 1) * span_rows] for i in range(2 * reach + 1)]

        def moved(block, by, further):
            moved_block = passed_on(block.astype(jnp.bfloat16), "seq", by, further)
            return moved_block.astype(jnp.float32)

        outer = after(jnp.stack([terms[0], terms[4]]).astype(jnp.bfloat16), ready)
        span_sums = terms[2] + moved(terms[3] + moved(outer[1], 1, 2), 1, 1)
        span_sums = span_sums + moved(terms[1] + moved(outer[0], -1, -2), -1, -1)
        return span_sums.astype(jnp.bfloat16)[None]

    window_grad = lax.all_gather(
        after(main_in_grad[0], own_weights[0]), "seq", axis=0, tiled=True
    )
    span_index = jnp.arange(window_grad.shape[0], dtype=jnp.int32)
    start_picker = ((span_of[:, None] == span_index[None, :]) & starts[:, None]).astype(jnp.bfloat16)
    start_grad = jnp.dot(start_picker, window_grad, preferred_element_type=jnp.float32)

    def partial(own_weight, other_weight):
        total = product(own_side, own_weight) + product(other_side, other_weight)
        return total.astype(jnp.bfloat16)

    pieces = []
    far_part, main_grad = None, None
    for own_weight in own_weights:
        if far_part is not None:
            own_weight = after(own_weight, far_part)
        other_weight = swapped(own_weight, "pipe")
        block_rows = own_weight.shape[0] // tensor_count
        if tensor_count == 2:

            def half(index):
                return [
                    lax.dynamic_slice_in_dim(weight, index * block_rows, block_rows, 0)
                    for weight in (own_weight, other_weight)
                ]

            far_part = partial(*half(1 - tensor_index))
            incoming = swapped(far_part, "tensor").astype(jnp.float32)
            total = partial(*half(tensor_index)).astype(jnp.float32) + incoming
        else:
            total = lax.psum_scatter(
                partial(own_weight, other_weight), "tensor", scatter_dimension=1, tiled=True
            ).astype(jnp.float32)
        own = total[:row_count]
        returned = total[row_count:].astype(jnp.bfloat16)
        if main_grad is None:
            main_grad = span_part(returned)
        arrived = swapped(returned, "groups").astype(jnp.float32)
        pieces.append(
            [jnp.where(group_index == 0, own, arrived), jnp.where(group_index == 0, arrived, own)]
        )
    widths = [high - low for low, high in cuts]
    routing = jnp.concatenate(
        [
            piece[group][:, s * width : (s + 1) * width]
            for s in range(seq_count // tensor_count)
            for group in range(2)
            for piece, width in zip(pieces, widths)
        ],
        1,
    )
    byte_grad = (cotangent_wide + start_grad + routing).astype(jnp.bfloat16)[None]
    return (byte_grad, main_grad)


def solution(mesh):
    return jax.shard_map(
        shards,
        mesh=mesh,
        in_specs=(
            P(("groups", "pipe"), "seq", "tensor"),
            P(("groups", "pipe"), "seq", "tensor"),
            P(("groups", "pipe"), "seq", "tensor"),
            P(("groups", "pipe"), "seq", "tensor"),
            P(("groups", "pipe"), "seq", "tensor"),
            P(("groups", "pipe"), None),
            P("seq", "tensor"),
            P("seq", "tensor"),
        ),
        out_specs=(P(("groups", "pipe"), "seq", "tensor"), P(("groups", "pipe"), "seq", "tensor")),
        check_vma=False,
    )
```

```python
import jax
import jax.numpy as jnp
from jax import lax
from jax.experimental import pallas as pl
from jax.experimental.pallas import tpu as pltpu
from jax.sharding import PartitionSpec as P

epsilon = 1e-06


def passed_along(x, axis, by):
    length = lax.axis_size(axis)
    pairs = [(i, i + by) for i in range(length) if 0 <= i + by < length]
    return lax.ppermute(x, axis, pairs)


reach = 2


def swapped(x, axis):
    length = lax.axis_size(axis)
    return lax.ppermute(x, axis, [(i, length - 1 - i) for i in range(length)])


def passed_on(x, axis, by, came_from):
    length = lax.axis_size(axis)
    pairs = [
        (i, i + by) for i in range(length) if 0 <= i + by < length and 0 <= i + came_from < length
    ]
    return lax.ppermute(x, axis, pairs)


def after(value, *others):
    def kernel(*refs):
        del refs

    anywhere = pl.BlockSpec(memory_space=pl.ANY)
    return pl.pallas_call(
        kernel,
        out_shape=jax.ShapeDtypeStruct(value.shape, value.dtype),
        in_specs=[anywhere] * (1 + len(others)),
        out_specs=anywhere,
        input_output_aliases={0: 0},
        name="after",
    )(value, *others)


def byte_sums_kernel(shard_ref, bounds_ref, cotangent_ref, query_ref, key_ref, *refs):
    blocks, out_ref = refs[:-1], refs[-1]
    rows, width = query_ref.shape
    span_rows = blocks[reach].shape[0]
    shard = shard_ref[0]
    row = lax.broadcasted_iota(jnp.int32, (rows, 1), 0)
    held = (bounds_ref[...] <= shard * rows + row).astype(jnp.float32)
    span_of = jnp.sum(held, 1, keepdims=True).astype(jnp.int32) - 1
    place = span_of - (shard - reach) * span_rows
    column = lax.broadcasted_iota(jnp.int32, (rows, span_rows), 1)
    pickers = [
        (place - i * span_rows == column).astype(jnp.float32).astype(jnp.bfloat16)
        for i in range(len(blocks))
    ]
    last_row = blocks[reach - 1].shape[0] - 1
    tile = 384
    totals = [jnp.zeros((rows, 128), jnp.float32)] * 4
    for start in range(0, width, tile):
        cols = pl.ds(start, tile)
        upsampled = jnp.zeros((rows, tile), jnp.float32)
        for picker, block in zip(pickers, blocks):
            upsampled = upsampled + jnp.dot(
                picker, block[:span_rows, cols], preferred_element_type=jnp.float32
            )
        query = query_ref[:, cols].astype(jnp.float32)
        previous = pltpu.roll(key_ref[:, cols].astype(jnp.float32), 1, 0)
        edge = blocks[reach - 1][last_row - 15 :, cols].astype(jnp.float32)[15:16]
        previous = jnp.where(row == 0, edge, previous)
        cotangent = cotangent_ref[:, cols].astype(jnp.float32)
        terms = [query * previous, query * query, previous * previous, cotangent * upsampled]
        for piece in range(0, tile, 128):
            totals = [
                total + term[:, piece : piece + 128] for total, term in zip(totals, terms)
            ]
    lines = [jnp.sum(total.T, 0, keepdims=True) for total in totals]
    out_ref[...] = jnp.concatenate(lines + [jnp.zeros((4, rows), jnp.float32)], 0)


def byte_sums(shard_index, bounds, cotangent, query_rows, key_rows, blocks):
    rows = query_rows.shape[0]
    vmem = pl.BlockSpec(memory_space=pltpu.VMEM)
    return pl.pallas_call(
        byte_sums_kernel,
        out_shape=jax.ShapeDtypeStruct((8, rows), jnp.float32),
        in_specs=[pl.BlockSpec(memory_space=pltpu.SMEM)] + [vmem] * (4 + len(blocks)),
        out_specs=vmem,
        compiler_params=pltpu.CompilerParams(vmem_limit_bytes=40 * 1024 * 1024),
        name="byte_sums",
    )(shard_index[None], bounds, cotangent, query_rows, key_rows, *blocks)


def product(rows, weight):
    return lax.dot_general(
        rows, weight, (((1,), (1,)), ((), ())), preferred_element_type=jnp.float32
    )


def shards(out_grad, queries, keys, main_out, main_in_grad, boundaries, query_weight, key_weight):
    cotangent = out_grad[0]
    query_rows = queries[0]
    key_rows = keys[0]
    bounds_row = boundaries[0]
    row_count = cotangent.shape[0]
    span_rows = main_out.shape[1]
    shard_index = lax.axis_index("seq")
    seq_count = lax.axis_size("seq")
    tensor_count = lax.axis_size("tensor")
    tensor_index = lax.axis_index("tensor")
    group_index = lax.axis_index("groups")
    pipe_index = lax.axis_index("pipe")
    group_rows = query_weight.shape[0] // lax.axis_size("groups")
    half_cols = query_weight.shape[1] // lax.axis_size("pipe")

    def columns(x, index):
        return lax.dynamic_slice_in_dim(x, index * half_cols, half_cols, 1)

    own_piece = jnp.concatenate(
        [
            lax.dynamic_slice(
                weight, (group_index * group_rows, pipe_index * half_cols), (group_rows, half_cols)
            )
            for weight in (query_weight, key_weight)
        ],
        1,
    )
    own_weight = lax.all_gather(own_piece, "seq", axis=0, tiled=True)
    out_right = passed_along(jnp.concatenate([main_out[0], key_rows[-16:]], 0), "seq", 1)
    out_left = passed_along(jnp.concatenate([main_out[0], query_rows[:16]], 0), "seq", -1)
    out_far_right = passed_along(main_out[0], "seq", 2)
    out_far_left = passed_along(main_out[0], "seq", -2)
    query_other = swapped(query_rows, "groups")
    key_other = swapped(key_rows, "groups")
    last_key, next_query = out_right[-1:], out_left[span_rows : span_rows + 1]
    edges_other = swapped(jnp.concatenate([last_key, next_query], 0), "groups")
    last_key_other, next_query_other = edges_other[:1], edges_other[1:]
    blocks = [out_far_right, out_right, main_out[0], out_left, out_far_left]
    sums = byte_sums(shard_index, boundaries, cotangent, query_rows, key_rows, blocks)

    positions = shard_index * row_count + jnp.arange(row_count, dtype=jnp.int32)
    span_of = jnp.sum((bounds_row[None, :] <= positions[:, None]).astype(jnp.int32), 1) - 1
    starts = jnp.any(bounds_row[None, :] == positions[:, None], 1)
    place = span_of - (shard_index - reach) * span_rows
    window_rows = (2 * reach + 1) * span_rows
    selector = place[:, None] == jnp.arange(window_rows, dtype=jnp.int32)[None, :]
    cotangent_wide = cotangent.astype(jnp.float32)
    if tensor_count == 2:
        sums = sums + swapped(sums, "tensor")
    else:
        sums = lax.psum(sums, "tensor")
    cross_sum, query_sum, key_sum, conf_grad = sums[:4]
    query_scale = lax.rsqrt(query_sum + epsilon)
    key_scale = lax.rsqrt(key_sum + epsilon)
    cosine = cross_sum * query_scale * key_scale
    probability = jnp.where(positions == 0, 1.0, 0.5 * (1.0 - cosine))
    confidence = jnp.where(starts, probability, 1.0 - probability)
    sign = jnp.where(starts, 1.0, -1.0)
    cos_grad = jnp.where(positions == 0, 0.0, -0.5 * sign * conf_grad)
    factors = jnp.stack(
        [
            cos_grad * (query_scale * key_scale),
            cos_grad * (cosine * query_scale * query_scale),
            cos_grad * (cosine * key_scale * key_scale),
        ]
    )
    next_factors = passed_along(factors[:, :1], "seq", -1)
    factors = jnp.concatenate([factors, next_factors], 1)
    factors_other = swapped(factors, "groups")

    def grads(queries_here, keys_here, key_before, query_after, here, index):
        previous = jnp.concatenate([columns(key_before, index), columns(keys_here, index)[:-1]], 0)
        current = columns(queries_here, index)
        following = jnp.concatenate([current[1:], columns(query_after, index)], 0)
        ahead, here = here[:, 1:], here[:, :-1]
        query_grad = here[0][:, None] * previous.astype(jnp.float32)
        query_grad = query_grad - here[1][:, None] * current.astype(jnp.float32)
        key_grad = ahead[0][:, None] * following.astype(jnp.float32)
        key_grad = key_grad - ahead[2][:, None] * columns(keys_here, index).astype(jnp.float32)
        return jnp.concatenate([query_grad.astype(jnp.bfloat16), key_grad.astype(jnp.bfloat16)], 1)

    own_tokens = (query_rows, key_rows, last_key, next_query, factors)
    other_tokens = (query_other, key_other, last_key_other, next_query_other, factors_other)
    own_sides = [grads(*own_tokens, pipe_index), grads(*own_tokens, 1 - pipe_index)]
    other_sides = [grads(*other_tokens, pipe_index), grads(*other_tokens, 1 - pipe_index)]

    def span_part(ready):
        conf_high = confidence.astype(jnp.bfloat16)
        conf_low = (confidence - conf_high.astype(jnp.float32)).astype(jnp.bfloat16)
        zero_weight = jnp.zeros((), jnp.bfloat16)
        weight_high = jnp.where(selector, conf_high[:, None], zero_weight)
        weight_low = jnp.where(selector, conf_low[:, None], zero_weight)
        contract = (((0,), (0,)), ((), ()))
        span_terms = lax.dot_general(
            weight_high, cotangent, contract, preferred_element_type=jnp.float32
        )
        span_terms = span_terms + lax.dot_general(
            weight_low, cotangent, contract, preferred_element_type=jnp.float32
        )
        terms = [span_terms[i * span_rows : (i + 1) * span_rows] for i in range(2 * reach + 1)]

        def moved(block, by, further):
            moved_block = passed_on(block.astype(jnp.bfloat16), "seq", by, further)
            return moved_block.astype(jnp.float32)

        outer = after(jnp.stack([terms[0], terms[4]]).astype(jnp.bfloat16), ready)
        span_sums = terms[2] + moved(terms[3] + moved(outer[1], 1, 2), 1, 1)
        span_sums = span_sums + moved(terms[1] + moved(outer[0], -1, -2), -1, -1)
        return span_sums.astype(jnp.bfloat16)[None]

    window_grad = lax.all_gather(
        after(main_in_grad[0], factors_other), "seq", axis=0, tiled=True
    )
    span_index = jnp.arange(window_grad.shape[0], dtype=jnp.int32)
    start_picker = ((span_of[:, None] == span_index[None, :]) & starts[:, None]).astype(jnp.bfloat16)
    start_grad = jnp.dot(start_picker, window_grad, preferred_element_type=jnp.float32)

    main_grad = span_part(factors_other)

    def partial(sides, weights):
        total = product(sides[0], weights[0]) + product(sides[1], weights[1])
        return total.astype(jnp.bfloat16)

    block_rows = own_weight.shape[0] // tensor_count
    if tensor_count == 2:

        def both(index):
            own = lax.dynamic_slice_in_dim(own_weight, index * block_rows, block_rows, 0)
            return own, swapped(own, "pipe")

        far, near = both(1 - tensor_index), both(tensor_index)
        other_far = swapped(partial(other_sides, far), "tensor")
        own_far = swapped(partial(own_sides, far), "tensor")
        other_sum = partial(other_sides, near).astype(jnp.float32) + other_far.astype(jnp.float32)
        own_sum = partial(own_sides, near).astype(jnp.float32) + own_far.astype(jnp.float32)
    else:
        weights = own_weight, swapped(own_weight, "pipe")
        other_sum, own_sum = [
            lax.psum_scatter(
                partial(sides, weights), "tensor", scatter_dimension=1, tiled=True
            ).astype(jnp.float32)
            for sides in (other_sides, own_sides)
        ]
    arrived = swapped(other_sum.astype(jnp.bfloat16), "groups").astype(jnp.float32)
    first = jnp.where(group_index == 0, own_sum, arrived)
    second = jnp.where(group_index == 0, arrived, own_sum)
    routing = jnp.concatenate(
        [
            side[:, low : low + group_rows]
            for low in range(0, block_rows, group_rows)
            for side in (first, second)
        ],
        1,
    )
    byte_grad = (cotangent_wide + start_grad + routing).astype(jnp.bfloat16)[None]
    return (byte_grad, main_grad)


def solution(mesh):
    return jax.shard_map(
        shards,
        mesh=mesh,
        in_specs=(
            P(("groups", "pipe"), "seq", "tensor"),
            P(("groups", "pipe"), "seq", "tensor"),
            P(("groups", "pipe"), "seq", "tensor"),
            P(("groups", "pipe"), "seq", "tensor"),
            P(("groups", "pipe"), "seq", "tensor"),
            P(("groups", "pipe"), None),
            P("seq", "tensor"),
            P("seq", "tensor"),
        ),
        out_specs=(P(("groups", "pipe"), "seq", "tensor"), P(("groups", "pipe"), "seq", "tensor")),
        check_vma=False,
    )
```

```python
import jax
import jax.numpy as jnp
from jax import lax
from jax.experimental import pallas as pl
from jax.experimental.pallas import tpu as pltpu
from jax.sharding import PartitionSpec as P

epsilon = 1e-06


def passed_along(x, axis, by):
    length = lax.axis_size(axis)
    pairs = [(i, i + by) for i in range(length) if 0 <= i + by < length]
    return lax.ppermute(x, axis, pairs)


reach = 2


def swapped(x, axis):
    length = lax.axis_size(axis)
    return lax.ppermute(x, axis, [(i, length - 1 - i) for i in range(length)])


def after(value, *others):
    def kernel(*refs):
        del refs

    anywhere = pl.BlockSpec(memory_space=pl.ANY)
    return pl.pallas_call(
        kernel,
        out_shape=jax.ShapeDtypeStruct(value.shape, value.dtype),
        in_specs=[anywhere] * (1 + len(others)),
        out_specs=anywhere,
        input_output_aliases={0: 0},
        name="after",
    )(value, *others)


def byte_sums_kernel(shard_ref, bounds_ref, cotangent_ref, query_ref, key_ref, *refs):
    blocks, out_ref = refs[:-1], refs[-1]
    rows, width = query_ref.shape
    span_rows = blocks[reach].shape[0]
    shard = shard_ref[0]
    row = lax.broadcasted_iota(jnp.int32, (rows, 1), 0)
    held = (bounds_ref[...] <= shard * rows + row).astype(jnp.float32)
    span_of = jnp.sum(held, 1, keepdims=True).astype(jnp.int32) - 1
    place = span_of - (shard - reach) * span_rows
    column = lax.broadcasted_iota(jnp.int32, (rows, span_rows), 1)
    pickers = [
        (place - i * span_rows == column).astype(jnp.float32).astype(jnp.bfloat16)
        for i in range(len(blocks))
    ]
    last_row = blocks[reach - 1].shape[0] - 1
    tile = 384
    totals = [jnp.zeros((rows, 128), jnp.float32)] * 4
    for start in range(0, width, tile):
        cols = pl.ds(start, tile)
        upsampled = jnp.zeros((rows, tile), jnp.float32)
        for picker, block in zip(pickers, blocks):
            upsampled = upsampled + jnp.dot(
                picker, block[:span_rows, cols], preferred_element_type=jnp.float32
            )
        query = query_ref[:, cols].astype(jnp.float32)
        previous = pltpu.roll(key_ref[:, cols].astype(jnp.float32), 1, 0)
        edge = blocks[reach - 1][last_row - 15 :, cols].astype(jnp.float32)[15:16]
        previous = jnp.where(row == 0, edge, previous)
        cotangent = cotangent_ref[:, cols].astype(jnp.float32)
        terms = [query * previous, query * query, previous * previous, cotangent * upsampled]
        for piece in range(0, tile, 128):
            totals = [
                total + term[:, piece : piece + 128] for total, term in zip(totals, terms)
            ]
    lines = [jnp.sum(total.T, 0, keepdims=True) for total in totals]
    out_ref[...] = jnp.concatenate(lines + [jnp.zeros((4, rows), jnp.float32)], 0)


def byte_sums(shard_index, bounds, cotangent, query_rows, key_rows, blocks):
    rows = query_rows.shape[0]
    vmem = pl.BlockSpec(memory_space=pltpu.VMEM)
    return pl.pallas_call(
        byte_sums_kernel,
        out_shape=jax.ShapeDtypeStruct((8, rows), jnp.float32),
        in_specs=[pl.BlockSpec(memory_space=pltpu.SMEM)] + [vmem] * (4 + len(blocks)),
        out_specs=vmem,
        compiler_params=pltpu.CompilerParams(vmem_limit_bytes=40 * 1024 * 1024),
        name="byte_sums",
    )(shard_index[None], bounds, cotangent, query_rows, key_rows, *blocks)


def base_kernel(shard_ref, bounds_ref, cotangent_ref, *refs):
    blocks, out_ref = refs[:-1], refs[-1]
    rows, width = cotangent_ref.shape
    span_rows = blocks[reach].shape[0]
    shard = shard_ref[0]
    position = shard * rows + lax.broadcasted_iota(jnp.int32, (rows, 1), 0)
    held = (bounds_ref[...] <= position).astype(jnp.float32)
    held_before = (bounds_ref[...] < position).astype(jnp.float32)
    count = jnp.sum(held, 1, keepdims=True)
    starts = count > jnp.sum(held_before, 1, keepdims=True)
    place = count.astype(jnp.int32) - 1 - (shard - reach) * span_rows
    place = jnp.where(starts, place, -1)
    column = lax.broadcasted_iota(jnp.int32, (rows, span_rows), 1)
    pickers = [
        (place - i * span_rows == column).astype(jnp.float32).astype(jnp.bfloat16)
        for i in range(len(blocks))
    ]
    tile = 384
    for start in range(0, width, tile):
        cols = pl.ds(start, tile)
        total = cotangent_ref[:, cols].astype(jnp.float32)
        for picker, block in zip(pickers, blocks):
            total = total + jnp.dot(
                picker, block[:span_rows, cols], preferred_element_type=jnp.float32
            )
        out_ref[:, cols] = total


def base_of(shard_index, bounds, cotangent, blocks):
    vmem = pl.BlockSpec(memory_space=pltpu.VMEM)
    return pl.pallas_call(
        base_kernel,
        out_shape=jax.ShapeDtypeStruct(cotangent.shape, jnp.float32),
        in_specs=[pl.BlockSpec(memory_space=pltpu.SMEM)] + [vmem] * (2 + len(blocks)),
        out_specs=vmem,
        compiler_params=pltpu.CompilerParams(vmem_limit_bytes=40 * 1024 * 1024),
        name="base",
    )(shard_index[None], bounds, cotangent, *blocks)


def product(rows, weight):
    return lax.dot_general(
        rows, weight, (((1,), (1,)), ((), ())), preferred_element_type=jnp.float32
    )


def shards(out_grad, queries, keys, main_out, main_in_grad, boundaries, query_weight, key_weight):
    cotangent = out_grad[0]
    query_rows = queries[0]
    key_rows = keys[0]
    bounds_row = boundaries[0]
    row_count = cotangent.shape[0]
    span_rows = main_out.shape[1]
    shard_index = lax.axis_index("seq")
    seq_count = lax.axis_size("seq")
    tensor_count = lax.axis_size("tensor")
    tensor_index = lax.axis_index("tensor")
    group_index = lax.axis_index("groups")
    pipe_index = lax.axis_index("pipe")
    group_rows = query_weight.shape[0] // lax.axis_size("groups")
    half_cols = query_weight.shape[1] // lax.axis_size("pipe")

    def columns(x, index):
        return lax.dynamic_slice_in_dim(x, index * half_cols, half_cols, 1)

    first_rows = group_rows * 2 // 3 // 16 * 16
    cuts = [(0, first_rows), (first_rows, group_rows)]
    out_right = passed_along(jnp.concatenate([main_out[0], key_rows[-16:]], 0), "seq", 1)
    out_left = passed_along(jnp.concatenate([main_out[0], query_rows[:16]], 0), "seq", -1)
    out_far_right = passed_along(main_out[0], "seq", 2)
    out_far_left = passed_along(main_out[0], "seq", -2)
    rows_other = swapped(jnp.concatenate([query_rows, key_rows], 0), "groups")
    query_other, key_other = rows_other[:row_count], rows_other[row_count:]
    own_weights = []
    for low, high in cuts:
        piece = jnp.concatenate(
            [
                lax.dynamic_slice(
                    weight,
                    (group_index * group_rows + low, pipe_index * half_cols),
                    (high - low, half_cols),
                )
                for weight in (query_weight, key_weight)
            ],
            1,
        )
        if own_weights:
            piece = after(piece, out_right)
        own_weights.append(lax.all_gather(piece, "seq", axis=0, tiled=True))
    last_key, next_query = out_right[-1:], out_left[span_rows : span_rows + 1]
    edges_other = swapped(jnp.concatenate([last_key, next_query], 0), "groups")
    last_key_other, next_query_other = edges_other[:1], edges_other[1:]
    blocks = [out_far_right, out_right, main_out[0], out_left, out_far_left]
    sums = byte_sums(shard_index, boundaries, cotangent, query_rows, key_rows, blocks)

    positions = shard_index * row_count + jnp.arange(row_count, dtype=jnp.int32)
    span_of = jnp.sum((bounds_row[None, :] <= positions[:, None]).astype(jnp.int32), 1) - 1
    starts = jnp.any(bounds_row[None, :] == positions[:, None], 1)
    place = span_of - (shard_index - reach) * span_rows
    window_rows = (2 * reach + 1) * span_rows
    selector = place[:, None] == jnp.arange(window_rows, dtype=jnp.int32)[None, :]
    if tensor_count == 2:
        sums = sums + swapped(sums, "tensor")
    else:
        sums = lax.psum(sums, "tensor")
    cross_sum, query_sum, key_sum, conf_grad = sums[:4]
    query_scale = lax.rsqrt(query_sum + epsilon)
    key_scale = lax.rsqrt(key_sum + epsilon)
    cosine = cross_sum * query_scale * key_scale
    probability = jnp.where(positions == 0, 1.0, 0.5 * (1.0 - cosine))
    confidence = jnp.where(starts, probability, 1.0 - probability)
    sign = jnp.where(starts, 1.0, -1.0)
    cos_grad = jnp.where(positions == 0, 0.0, -0.5 * sign * conf_grad)
    factors = jnp.stack(
        [
            cos_grad * (query_scale * key_scale),
            cos_grad * (cosine * query_scale * query_scale),
            cos_grad * (cosine * key_scale * key_scale),
        ]
    )
    next_factors = passed_along(factors[:, :1], "seq", -1)
    factors = jnp.concatenate([factors, next_factors], 1)
    factors_other = swapped(factors, "groups")

    def grads(queries_here, keys_here, key_before, query_after, here, index):
        previous = jnp.concatenate([columns(key_before, index), columns(keys_here, index)[:-1]], 0)
        current = columns(queries_here, index)
        following = jnp.concatenate([current[1:], columns(query_after, index)], 0)
        ahead, here = here[:, 1:], here[:, :-1]
        query_grad = here[0][:, None] * previous.astype(jnp.float32)
        query_grad = query_grad - here[1][:, None] * current.astype(jnp.float32)
        key_grad = ahead[0][:, None] * following.astype(jnp.float32)
        key_grad = key_grad - ahead[2][:, None] * columns(keys_here, index).astype(jnp.float32)
        return jnp.concatenate([query_grad.astype(jnp.bfloat16), key_grad.astype(jnp.bfloat16)], 1)

    def both_grads(index):
        own = grads(query_rows, key_rows, last_key, next_query, factors, index)
        other = grads(
            query_other,
            key_other,
            last_key_other,
            next_query_other,
            factors_other,
            index,
        )
        return jnp.concatenate([own, other], 0)

    own_side, other_side = both_grads(pipe_index), both_grads(1 - pipe_index)

    def span_part(ready):
        conf_high = confidence.astype(jnp.bfloat16)
        conf_low = (confidence - conf_high.astype(jnp.float32)).astype(jnp.bfloat16)
        zero_weight = jnp.zeros((), jnp.bfloat16)
        weight_high = jnp.where(selector, conf_high[:, None], zero_weight)
        weight_low = jnp.where(selector, conf_low[:, None], zero_weight)
        contract = (((0,), (0,)), ((), ()))
        span_terms = lax.dot_general(
            weight_high, cotangent, contract, preferred_element_type=jnp.float32
        )
        span_terms = span_terms + lax.dot_general(
            weight_low, cotangent, contract, preferred_element_type=jnp.float32
        )
        terms = [span_terms[i * span_rows : (i + 1) * span_rows] for i in range(2 * reach + 1)]

        def sent(i):
            block = jnp.concatenate([main_in_grad[0], terms[i].astype(jnp.bfloat16)], 0)
            return passed_along(after(block, ready), "seq", i - reach)

        right, left, far_right, far_left = sent(3), sent(1), sent(4), sent(0)
        span_sums = terms[reach]
        for block in (right, left, far_right, far_left):
            span_sums = span_sums + block[span_rows:].astype(jnp.float32)
        base = base_of(
            shard_index,
            boundaries,
            cotangent,
            [far_right, right, main_in_grad[0], left, far_left],
        )
        return span_sums.astype(jnp.bfloat16)[None], base

    def partial(own_weight, other_weight):
        total = product(own_side, own_weight) + product(other_side, other_weight)
        return total.astype(jnp.bfloat16)

    pieces = []
    far_part, main_grad, base = None, None, None
    for own_weight in own_weights:
        if far_part is not None:
            own_weight = after(own_weight, far_part)
        other_weight = swapped(own_weight, "pipe")
        block_rows = own_weight.shape[0] // tensor_count
        if tensor_count == 2:

            def half(index):
                return [
                    lax.dynamic_slice_in_dim(weight, index * block_rows, block_rows, 0)
                    for weight in (own_weight, other_weight)
                ]

            far_part = partial(*half(1 - tensor_index))
            if base is None:
                main_grad, base = span_part(far_part)
            incoming = swapped(far_part, "tensor").astype(jnp.float32)
            total = partial(*half(tensor_index)).astype(jnp.float32) + incoming
        else:
            far_part = partial(own_weight, other_weight)
            if base is None:
                main_grad, base = span_part(far_part)
            total = lax.psum_scatter(
                far_part, "tensor", scatter_dimension=1, tiled=True
            ).astype(jnp.float32)
        own = total[:row_count]
        returned = total[row_count:].astype(jnp.bfloat16)
        arrived = swapped(returned, "groups").astype(jnp.float32)
        pieces.append(
            [jnp.where(group_index == 0, own, arrived), jnp.where(group_index == 0, arrived, own)]
        )
    widths = [high - low for low, high in cuts]
    routing = jnp.concatenate(
        [
            piece[group][:, s * width : (s + 1) * width]
            for s in range(seq_count // tensor_count)
            for group in range(2)
            for piece, width in zip(pieces, widths)
        ],
        1,
    )
    byte_grad = (base + routing).astype(jnp.bfloat16)[None]
    return (byte_grad, main_grad)


def solution(mesh):
    return jax.shard_map(
        shards,
        mesh=mesh,
        in_specs=(
            P(("groups", "pipe"), "seq", "tensor"),
            P(("groups", "pipe"), "seq", "tensor"),
            P(("groups", "pipe"), "seq", "tensor"),
            P(("groups", "pipe"), "seq", "tensor"),
            P(("groups", "pipe"), "seq", "tensor"),
            P(("groups", "pipe"), None),
            P("seq", "tensor"),
            P("seq", "tensor"),
        ),
        out_specs=(P(("groups", "pipe"), "seq", "tensor"), P(("groups", "pipe"), "seq", "tensor")),
        check_vma=False,
    )
```

```python
import jax
import jax.numpy as jnp
from jax import lax
from jax.experimental import pallas as pl
from jax.experimental.pallas import tpu as pltpu
from jax.sharding import PartitionSpec as P

epsilon = 1e-06


def passed_along(x, axis, by):
    length = lax.axis_size(axis)
    pairs = [(i, i + by) for i in range(length) if 0 <= i + by < length]
    return lax.ppermute(x, axis, pairs)


reach = 2


def swapped(x, axis):
    length = lax.axis_size(axis)
    return lax.ppermute(x, axis, [(i, length - 1 - i) for i in range(length)])


def passed_on(x, axis, by, came_from):
    length = lax.axis_size(axis)
    pairs = [
        (i, i + by) for i in range(length) if 0 <= i + by < length and 0 <= i + came_from < length
    ]
    return lax.ppermute(x, axis, pairs)


def after(value, *others):
    def kernel(*refs):
        del refs

    anywhere = pl.BlockSpec(memory_space=pl.ANY)
    return pl.pallas_call(
        kernel,
        out_shape=jax.ShapeDtypeStruct(value.shape, value.dtype),
        in_specs=[anywhere] * (1 + len(others)),
        out_specs=anywhere,
        input_output_aliases={0: 0},
        name="after",
    )(value, *others)


def byte_sums_kernel(shard_ref, bounds_ref, cotangent_ref, query_ref, key_ref, *refs):
    blocks, out_ref = refs[:-1], refs[-1]
    rows, width = query_ref.shape
    span_rows = blocks[reach].shape[0] // 2
    shard = shard_ref[0]
    row = lax.broadcasted_iota(jnp.int32, (rows, 1), 0)
    held = (bounds_ref[...] <= shard * rows + row).astype(jnp.float32)
    span_of = jnp.sum(held, 1, keepdims=True).astype(jnp.int32) - 1
    place = span_of - (shard - reach) * span_rows
    column = lax.broadcasted_iota(jnp.int32, (rows, span_rows), 1)
    pickers = [
        (place - i * span_rows == column).astype(jnp.float32).astype(jnp.bfloat16)
        for i in range(len(blocks))
    ]
    last_row = blocks[reach - 1].shape[0] - 1
    tile = 384
    totals = [jnp.zeros((rows, 128), jnp.float32)] * 4
    for start in range(0, width, tile):
        cols = pl.ds(start, tile)
        upsampled = jnp.zeros((rows, tile), jnp.float32)
        for picker, block in zip(pickers, blocks):
            upsampled = upsampled + jnp.dot(
                picker, block[:span_rows, cols], preferred_element_type=jnp.float32
            )
        query = query_ref[:, cols].astype(jnp.float32)
        previous = pltpu.roll(key_ref[:, cols].astype(jnp.float32), 1, 0)
        edge = blocks[reach - 1][last_row - 15 :, cols].astype(jnp.float32)[15:16]
        previous = jnp.where(row == 0, edge, previous)
        cotangent = cotangent_ref[:, cols].astype(jnp.float32)
        terms = [query * previous, query * query, previous * previous, cotangent * upsampled]
        for piece in range(0, tile, 128):
            totals = [
                total + term[:, piece : piece + 128] for total, term in zip(totals, terms)
            ]
    lines = [jnp.sum(total.T, 0, keepdims=True) for total in totals]
    out_ref[...] = jnp.concatenate(lines + [jnp.zeros((4, rows), jnp.float32)], 0)


def byte_sums(shard_index, bounds, cotangent, query_rows, key_rows, blocks):
    rows = query_rows.shape[0]
    vmem = pl.BlockSpec(memory_space=pltpu.VMEM)
    return pl.pallas_call(
        byte_sums_kernel,
        out_shape=jax.ShapeDtypeStruct((8, rows), jnp.float32),
        in_specs=[pl.BlockSpec(memory_space=pltpu.SMEM)] + [vmem] * (4 + len(blocks)),
        out_specs=vmem,
        compiler_params=pltpu.CompilerParams(vmem_limit_bytes=40 * 1024 * 1024),
        name="byte_sums",
    )(shard_index[None], bounds, cotangent, query_rows, key_rows, *blocks)


def base_kernel(shard_ref, bounds_ref, cotangent_ref, *refs):
    blocks, out_ref = refs[:-1], refs[-1]
    rows, width = cotangent_ref.shape
    span_rows = blocks[reach].shape[0] // 2
    shard = shard_ref[0]
    position = shard * rows + lax.broadcasted_iota(jnp.int32, (rows, 1), 0)
    held = (bounds_ref[...] <= position).astype(jnp.float32)
    held_before = (bounds_ref[...] < position).astype(jnp.float32)
    count = jnp.sum(held, 1, keepdims=True)
    starts = count > jnp.sum(held_before, 1, keepdims=True)
    place = count.astype(jnp.int32) - 1 - (shard - reach) * span_rows
    place = jnp.where(starts, place, -1)
    column = lax.broadcasted_iota(jnp.int32, (rows, span_rows), 1)
    pickers = [
        (place - i * span_rows == column).astype(jnp.float32).astype(jnp.bfloat16)
        for i in range(len(blocks))
    ]
    tile = 384
    for start in range(0, width, tile):
        cols = pl.ds(start, tile)
        total = cotangent_ref[:, cols].astype(jnp.float32)
        for picker, block in zip(pickers, blocks):
            total = total + jnp.dot(
                picker, block[span_rows : 2 * span_rows, cols], preferred_element_type=jnp.float32
            )
        out_ref[:, cols] = total


def base_of(shard_index, bounds, cotangent, blocks):
    vmem = pl.BlockSpec(memory_space=pltpu.VMEM)
    return pl.pallas_call(
        base_kernel,
        out_shape=jax.ShapeDtypeStruct(cotangent.shape, jnp.float32),
        in_specs=[pl.BlockSpec(memory_space=pltpu.SMEM)] + [vmem] * (2 + len(blocks)),
        out_specs=vmem,
        compiler_params=pltpu.CompilerParams(vmem_limit_bytes=40 * 1024 * 1024),
        name="base",
    )(shard_index[None], bounds, cotangent, *blocks)


def product(rows, weight):
    return lax.dot_general(
        rows, weight, (((1,), (1,)), ((), ())), preferred_element_type=jnp.float32
    )


def shards(out_grad, queries, keys, main_out, main_in_grad, boundaries, query_weight, key_weight):
    cotangent = out_grad[0]
    query_rows = queries[0]
    key_rows = keys[0]
    bounds_row = boundaries[0]
    row_count = cotangent.shape[0]
    span_rows = main_out.shape[1]
    shard_index = lax.axis_index("seq")
    seq_count = lax.axis_size("seq")
    tensor_count = lax.axis_size("tensor")
    tensor_index = lax.axis_index("tensor")
    group_index = lax.axis_index("groups")
    pipe_index = lax.axis_index("pipe")
    group_rows = query_weight.shape[0] // lax.axis_size("groups")
    half_cols = query_weight.shape[1] // lax.axis_size("pipe")

    def columns(x, index):
        return lax.dynamic_slice_in_dim(x, index * half_cols, half_cols, 1)

    first_rows = group_rows * 2 // 3 // 16 * 16
    cuts = [(0, first_rows), (first_rows, group_rows)]
    pair = jnp.concatenate([main_out[0], main_in_grad[0]], 0)
    out_right = passed_along(jnp.concatenate([pair, key_rows[-16:]], 0), "seq", 1)
    out_left = passed_along(jnp.concatenate([pair, query_rows[:16]], 0), "seq", -1)
    out_far_right = passed_along(pair, "seq", 2)
    out_far_left = passed_along(pair, "seq", -2)
    rows_other = swapped(jnp.concatenate([query_rows, key_rows], 0), "groups")
    query_other, key_other = rows_other[:row_count], rows_other[row_count:]
    own_weights = []
    for low, high in cuts:
        piece = jnp.concatenate(
            [
                lax.dynamic_slice(
                    weight,
                    (group_index * group_rows + low, pipe_index * half_cols),
                    (high - low, half_cols),
                )
                for weight in (query_weight, key_weight)
            ],
            1,
        )
        if own_weights:
            piece = after(piece, out_right)
        own_weights.append(lax.all_gather(piece, "seq", axis=0, tiled=True))
    last_key, next_query = out_right[-1:], out_left[2 * span_rows : 2 * span_rows + 1]
    edges_other = swapped(jnp.concatenate([last_key, next_query], 0), "groups")
    last_key_other, next_query_other = edges_other[:1], edges_other[1:]
    blocks = [out_far_right, out_right, pair, out_left, out_far_left]
    sums = byte_sums(shard_index, boundaries, cotangent, query_rows, key_rows, blocks)

    positions = shard_index * row_count + jnp.arange(row_count, dtype=jnp.int32)
    span_of = jnp.sum((bounds_row[None, :] <= positions[:, None]).astype(jnp.int32), 1) - 1
    starts = jnp.any(bounds_row[None, :] == positions[:, None], 1)
    place = span_of - (shard_index - reach) * span_rows
    window_rows = (2 * reach + 1) * span_rows
    selector = place[:, None] == jnp.arange(window_rows, dtype=jnp.int32)[None, :]
    if tensor_count == 2:
        sums = sums + swapped(sums, "tensor")
    else:
        sums = lax.psum(sums, "tensor")
    cross_sum, query_sum, key_sum, conf_grad = sums[:4]
    query_scale = lax.rsqrt(query_sum + epsilon)
    key_scale = lax.rsqrt(key_sum + epsilon)
    cosine = cross_sum * query_scale * key_scale
    probability = jnp.where(positions == 0, 1.0, 0.5 * (1.0 - cosine))
    confidence = jnp.where(starts, probability, 1.0 - probability)
    sign = jnp.where(starts, 1.0, -1.0)
    cos_grad = jnp.where(positions == 0, 0.0, -0.5 * sign * conf_grad)
    factors = jnp.stack(
        [
            cos_grad * (query_scale * key_scale),
            cos_grad * (cosine * query_scale * query_scale),
            cos_grad * (cosine * key_scale * key_scale),
        ]
    )
    next_factors = passed_along(factors[:, :1], "seq", -1)
    factors = jnp.concatenate([factors, next_factors], 1)
    factors_other = swapped(factors, "groups")

    def grads(queries_here, keys_here, key_before, query_after, here, index):
        previous = jnp.concatenate([columns(key_before, index), columns(keys_here, index)[:-1]], 0)
        current = columns(queries_here, index)
        following = jnp.concatenate([current[1:], columns(query_after, index)], 0)
        ahead, here = here[:, 1:], here[:, :-1]
        query_grad = here[0][:, None] * previous.astype(jnp.float32)
        query_grad = query_grad - here[1][:, None] * current.astype(jnp.float32)
        key_grad = ahead[0][:, None] * following.astype(jnp.float32)
        key_grad = key_grad - ahead[2][:, None] * columns(keys_here, index).astype(jnp.float32)
        return jnp.concatenate([query_grad.astype(jnp.bfloat16), key_grad.astype(jnp.bfloat16)], 1)

    def both_grads(index):
        own = grads(query_rows, key_rows, last_key, next_query, factors, index)
        other = grads(
            query_other,
            key_other,
            last_key_other,
            next_query_other,
            factors_other,
            index,
        )
        return jnp.concatenate([own, other], 0)

    own_side, other_side = both_grads(pipe_index), both_grads(1 - pipe_index)

    def span_part(ready):
        conf_high = confidence.astype(jnp.bfloat16)
        conf_low = (confidence - conf_high.astype(jnp.float32)).astype(jnp.bfloat16)
        zero_weight = jnp.zeros((), jnp.bfloat16)
        weight_high = jnp.where(selector, conf_high[:, None], zero_weight)
        weight_low = jnp.where(selector, conf_low[:, None], zero_weight)
        contract = (((0,), (0,)), ((), ()))
        span_terms = lax.dot_general(
            weight_high, cotangent, contract, preferred_element_type=jnp.float32
        )
        span_terms = span_terms + lax.dot_general(
            weight_low, cotangent, contract, preferred_element_type=jnp.float32
        )
        terms = [span_terms[i * span_rows : (i + 1) * span_rows] for i in range(2 * reach + 1)]

        outer = after(jnp.stack([terms[0], terms[4]]).astype(jnp.bfloat16), ready)
        inner = jnp.stack(
            [
                terms[1] + passed_on(outer[0], "seq", -1, -2).astype(jnp.float32),
                terms[3] + passed_on(outer[1], "seq", 1, 2).astype(jnp.float32),
            ]
        )
        return terms[reach], inner.astype(jnp.bfloat16)

    base = base_of(shard_index, boundaries, cotangent, blocks)

    def partial(own_weight, other_weight):
        total = product(own_side, own_weight) + product(other_side, other_weight)
        return total.astype(jnp.bfloat16)

    pieces = []
    far_part, span_inner = None, None
    for own_weight in own_weights:
        if far_part is not None:
            own_weight = after(own_weight, far_part)
        other_weight = swapped(own_weight, "pipe")
        block_rows = own_weight.shape[0] // tensor_count
        if tensor_count == 2:

            def half(index):
                return [
                    lax.dynamic_slice_in_dim(weight, index * block_rows, block_rows, 0)
                    for weight in (own_weight, other_weight)
                ]

            far_part = partial(*half(1 - tensor_index))
            if span_inner is None:
                span_sums, span_inner = span_part(far_part)
            incoming = swapped(far_part, "tensor").astype(jnp.float32)
            total = partial(*half(tensor_index)).astype(jnp.float32) + incoming
        else:
            far_part = partial(own_weight, other_weight)
            if span_inner is None:
                span_sums, span_inner = span_part(far_part)
            total = lax.psum_scatter(
                far_part, "tensor", scatter_dimension=1, tiled=True
            ).astype(jnp.float32)
        own = total[:row_count]
        returned = total[row_count:].astype(jnp.bfloat16)
        arrived = swapped(returned, "groups").astype(jnp.float32)
        pieces.append(
            [jnp.where(group_index == 0, own, arrived), jnp.where(group_index == 0, arrived, own)]
        )
    span_inner = after(span_inner, far_part)
    span_sums = span_sums + passed_along(span_inner[0], "seq", -1).astype(jnp.float32)
    span_sums = span_sums + passed_along(span_inner[1], "seq", 1).astype(jnp.float32)
    main_grad = span_sums.astype(jnp.bfloat16)[None]
    widths = [high - low for low, high in cuts]
    routing = jnp.concatenate(
        [
            piece[group][:, s * width : (s + 1) * width]
            for s in range(seq_count // tensor_count)
            for group in range(2)
            for piece, width in zip(pieces, widths)
        ],
        1,
    )
    byte_grad = (base + routing).astype(jnp.bfloat16)[None]
    return (byte_grad, main_grad)


def solution(mesh):
    return jax.shard_map(
        shards,
        mesh=mesh,
        in_specs=(
            P(("groups", "pipe"), "seq", "tensor"),
            P(("groups", "pipe"), "seq", "tensor"),
            P(("groups", "pipe"), "seq", "tensor"),
            P(("groups", "pipe"), "seq", "tensor"),
            P(("groups", "pipe"), "seq", "tensor"),
            P(("groups", "pipe"), None),
            P("seq", "tensor"),
            P("seq", "tensor"),
        ),
        out_specs=(P(("groups", "pipe"), "seq", "tensor"), P(("groups", "pipe"), "seq", "tensor")),
        check_vma=False,
    )
```

```python
import jax
import jax.numpy as jnp
from jax import lax
from jax.experimental import pallas as pl
from jax.experimental.pallas import tpu as pltpu
from jax.sharding import PartitionSpec as P

epsilon = 1e-06


def passed_along(x, axis, by):
    length = lax.axis_size(axis)
    pairs = [(i, i + by) for i in range(length) if 0 <= i + by < length]
    return lax.ppermute(x, axis, pairs)


reach = 2


def swapped(x, axis):
    length = lax.axis_size(axis)
    return lax.ppermute(x, axis, [(i, length - 1 - i) for i in range(length)])


def passed_on(x, axis, by, came_from):
    length = lax.axis_size(axis)
    pairs = [
        (i, i + by) for i in range(length) if 0 <= i + by < length and 0 <= i + came_from < length
    ]
    return lax.ppermute(x, axis, pairs)


def second_neighbours(right, left):
    return passed_on(right, "seq", 1, -1), passed_on(left, "seq", -1, 1)


def after(value, *others):
    def kernel(*refs):
        del refs

    anywhere = pl.BlockSpec(memory_space=pl.ANY)
    return pl.pallas_call(
        kernel,
        out_shape=jax.ShapeDtypeStruct(value.shape, value.dtype),
        in_specs=[anywhere] * (1 + len(others)),
        out_specs=anywhere,
        input_output_aliases={0: 0},
        name="after",
    )(value, *others)


def byte_sums_kernel(shard_ref, bounds_ref, cotangent_ref, query_ref, key_ref, *refs):
    blocks, out_ref = refs[:-1], refs[-1]
    rows, width = query_ref.shape
    span_rows = blocks[reach].shape[0]
    shard = shard_ref[0]
    row = lax.broadcasted_iota(jnp.int32, (rows, 1), 0)
    held = (bounds_ref[...] <= shard * rows + row).astype(jnp.float32)
    span_of = jnp.sum(held, 1, keepdims=True).astype(jnp.int32) - 1
    place = span_of - (shard - reach) * span_rows
    column = lax.broadcasted_iota(jnp.int32, (rows, span_rows), 1)
    pickers = [
        (place - i * span_rows == column).astype(jnp.float32).astype(jnp.bfloat16)
        for i in range(len(blocks))
    ]
    last_row = blocks[reach - 1].shape[0] - 1
    tile = 384
    totals = [jnp.zeros((rows, 128), jnp.float32)] * 4
    for start in range(0, width, tile):
        cols = pl.ds(start, tile)
        upsampled = jnp.zeros((rows, tile), jnp.float32)
        for picker, block in zip(pickers, blocks):
            upsampled = upsampled + jnp.dot(
                picker, block[:span_rows, cols], preferred_element_type=jnp.float32
            )
        query = query_ref[:, cols].astype(jnp.float32)
        previous = pltpu.roll(key_ref[:, cols].astype(jnp.float32), 1, 0)
        edge = blocks[reach - 1][last_row - 15 :, cols].astype(jnp.float32)[15:16]
        previous = jnp.where(row == 0, edge, previous)
        cotangent = cotangent_ref[:, cols].astype(jnp.float32)
        terms = [query * previous, query * query, previous * previous, cotangent * upsampled]
        for piece in range(0, tile, 128):
            totals = [
                total + term[:, piece : piece + 128] for total, term in zip(totals, terms)
            ]
    lines = [jnp.sum(total.T, 0, keepdims=True) for total in totals]
    out_ref[...] = jnp.concatenate(lines + [jnp.zeros((4, rows), jnp.float32)], 0)


def byte_sums(shard_index, bounds, cotangent, query_rows, key_rows, blocks):
    rows = query_rows.shape[0]
    vmem = pl.BlockSpec(memory_space=pltpu.VMEM)
    return pl.pallas_call(
        byte_sums_kernel,
        out_shape=jax.ShapeDtypeStruct((8, rows), jnp.float32),
        in_specs=[pl.BlockSpec(memory_space=pltpu.SMEM)] + [vmem] * (4 + len(blocks)),
        out_specs=vmem,
        compiler_params=pltpu.CompilerParams(vmem_limit_bytes=40 * 1024 * 1024),
        name="byte_sums",
    )(shard_index[None], bounds, cotangent, query_rows, key_rows, *blocks)


def product(rows, weight):
    return lax.dot_general(
        rows, weight, (((1,), (1,)), ((), ())), preferred_element_type=jnp.float32
    )


def shards(out_grad, queries, keys, main_out, main_in_grad, boundaries, query_weight, key_weight):
    cotangent = out_grad[0]
    query_rows = queries[0]
    key_rows = keys[0]
    bounds_row = boundaries[0]
    row_count = cotangent.shape[0]
    span_rows = main_out.shape[1]
    shard_index = lax.axis_index("seq")
    seq_count = lax.axis_size("seq")
    tensor_count = lax.axis_size("tensor")
    tensor_index = lax.axis_index("tensor")
    group_index = lax.axis_index("groups")
    pipe_index = lax.axis_index("pipe")
    group_rows = query_weight.shape[0] // lax.axis_size("groups")
    half_cols = query_weight.shape[1] // lax.axis_size("pipe")

    def columns(x, index):
        return lax.dynamic_slice_in_dim(x, index * half_cols, half_cols, 1)

    first_rows = group_rows * 2 // 3 // 16 * 16
    cuts = [(0, first_rows), (first_rows, group_rows)]
    out_right = passed_along(jnp.concatenate([main_out[0], key_rows[-16:]], 0), "seq", 1)
    out_left = passed_along(jnp.concatenate([main_out[0], query_rows[:16]], 0), "seq", -1)
    query_other = swapped(query_rows, "groups")
    key_other = swapped(key_rows, "groups")
    own_weights = []
    for low, high in cuts:
        piece = jnp.concatenate(
            [
                lax.dynamic_slice(
                    weight,
                    (group_index * group_rows + low, pipe_index * half_cols),
                    (high - low, half_cols),
                )
                for weight in (query_weight, key_weight)
            ],
            1,
        )
        if own_weights:
            piece = after(piece, out_right)
        own_weights.append(lax.all_gather(piece, "seq", axis=0, tiled=True))
    out_far_right, out_far_left = second_neighbours(out_right, out_left)
    last_key, next_query = out_right[-1:], out_left[span_rows : span_rows + 1]
    edges_other = swapped(jnp.concatenate([last_key, next_query], 0), "groups")
    last_key_other, next_query_other = edges_other[:1], edges_other[1:]
    blocks = [out_far_right, out_right, main_out[0], out_left, out_far_left]
    sums = byte_sums(shard_index, boundaries, cotangent, query_rows, key_rows, blocks)

    positions = shard_index * row_count + jnp.arange(row_count, dtype=jnp.int32)
    span_of = jnp.sum((bounds_row[None, :] <= positions[:, None]).astype(jnp.int32), 1) - 1
    starts = jnp.any(bounds_row[None, :] == positions[:, None], 1)
    place = span_of - (shard_index - reach) * span_rows
    window_rows = (2 * reach + 1) * span_rows
    selector = place[:, None] == jnp.arange(window_rows, dtype=jnp.int32)[None, :]
    cotangent_wide = cotangent.astype(jnp.float32)
    if tensor_count == 2:
        sums = sums + swapped(sums, "tensor")
    else:
        sums = lax.psum(sums, "tensor")
    cross_sum, query_sum, key_sum, conf_grad = sums[:4]
    query_scale = lax.rsqrt(query_sum + epsilon)
    key_scale = lax.rsqrt(key_sum + epsilon)
    cosine = cross_sum * query_scale * key_scale
    probability = jnp.where(positions == 0, 1.0, 0.5 * (1.0 - cosine))
    confidence = jnp.where(starts, probability, 1.0 - probability)
    sign = jnp.where(starts, 1.0, -1.0)
    cos_grad = jnp.where(positions == 0, 0.0, -0.5 * sign * conf_grad)
    factors = jnp.stack(
        [
            cos_grad * (query_scale * key_scale),
            cos_grad * (cosine * query_scale * query_scale),
            cos_grad * (cosine * key_scale * key_scale),
        ]
    )
    next_factors = passed_along(factors[:, :1], "seq", -1)
    factors = jnp.concatenate([factors, next_factors], 1)
    factors_other = swapped(factors, "groups")

    def grads(queries_here, keys_here, key_before, query_after, here, index):
        previous = jnp.concatenate([columns(key_before, index), columns(keys_here, index)[:-1]], 0)
        current = columns(queries_here, index)
        following = jnp.concatenate([current[1:], columns(query_after, index)], 0)
        ahead, here = here[:, 1:], here[:, :-1]
        query_grad = here[0][:, None] * previous.astype(jnp.float32)
        query_grad = query_grad - here[1][:, None] * current.astype(jnp.float32)
        key_grad = ahead[0][:, None] * following.astype(jnp.float32)
        key_grad = key_grad - ahead[2][:, None] * columns(keys_here, index).astype(jnp.float32)
        return jnp.concatenate([query_grad.astype(jnp.bfloat16), key_grad.astype(jnp.bfloat16)], 1)

    def both_grads(index):
        own = grads(query_rows, key_rows, last_key, next_query, factors, index)
        other = grads(
            query_other,
            key_other,
            last_key_other,
            next_query_other,
            factors_other,
            index,
        )
        return jnp.concatenate([own, other], 0)

    own_side, other_side = both_grads(pipe_index), both_grads(1 - pipe_index)

    def span_part(ready):
        conf_high = confidence.astype(jnp.bfloat16)
        conf_low = (confidence - conf_high.astype(jnp.float32)).astype(jnp.bfloat16)
        zero_weight = jnp.zeros((), jnp.bfloat16)
        weight_high = jnp.where(selector, conf_high[:, None], zero_weight)
        weight_low = jnp.where(selector, conf_low[:, None], zero_weight)
        contract = (((0,), (0,)), ((), ()))
        span_terms = lax.dot_general(
            weight_high, cotangent, contract, preferred_element_type=jnp.float32
        )
        span_terms = span_terms + lax.dot_general(
            weight_low, cotangent, contract, preferred_element_type=jnp.float32
        )
        terms = [span_terms[i * span_rows : (i + 1) * span_rows] for i in range(2 * reach + 1)]

        def moved(block, by, further):
            moved_block = passed_on(block.astype(jnp.bfloat16), "seq", by, further)
            return moved_block.astype(jnp.float32)

        outer = after(jnp.stack([terms[0], terms[4]]).astype(jnp.bfloat16), ready)
        span_sums = terms[2] + moved(terms[3] + moved(outer[1], 1, 2), 1, 1)
        span_sums = span_sums + moved(terms[1] + moved(outer[0], -1, -2), -1, -1)
        return span_sums.astype(jnp.bfloat16)[None]

    window_grad = lax.all_gather(
        after(main_in_grad[0], own_weights[0]), "seq", axis=0, tiled=True
    )
    span_index = jnp.arange(window_grad.shape[0], dtype=jnp.int32)
    start_picker = ((span_of[:, None] == span_index[None, :]) & starts[:, None]).astype(jnp.bfloat16)
    start_grad = jnp.dot(start_picker, window_grad, preferred_element_type=jnp.float32)

    def partial(own_weight, other_weight):
        total = product(own_side, own_weight) + product(other_side, other_weight)
        return total.astype(jnp.bfloat16)

    pieces = []
    main_grad = span_part(factors_other)
    far_part = None
    for own_weight in own_weights:
        if far_part is not None:
            own_weight = after(own_weight, far_part)
        other_weight = swapped(own_weight, "pipe")
        block_rows = own_weight.shape[0] // tensor_count
        if tensor_count == 2:

            def half(index):
                return [
                    lax.dynamic_slice_in_dim(weight, index * block_rows, block_rows, 0)
                    for weight in (own_weight, other_weight)
                ]

            far_part = partial(*half(1 - tensor_index))
            incoming = swapped(far_part, "tensor").astype(jnp.float32)
            total = partial(*half(tensor_index)).astype(jnp.float32) + incoming
        else:
            total = lax.psum_scatter(
                partial(own_weight, other_weight), "tensor", scatter_dimension=1, tiled=True
            ).astype(jnp.float32)
        own = total[:row_count]
        returned = total[row_count:].astype(jnp.bfloat16)
        arrived = swapped(returned, "groups").astype(jnp.float32)
        pieces.append(
            [jnp.where(group_index == 0, own, arrived), jnp.where(group_index == 0, arrived, own)]
        )
    widths = [high - low for low, high in cuts]
    routing = jnp.concatenate(
        [
            piece[group][:, s * width : (s + 1) * width]
            for s in range(seq_count // tensor_count)
            for group in range(2)
            for piece, width in zip(pieces, widths)
        ],
        1,
    )
    byte_grad = (cotangent_wide + start_grad + routing).astype(jnp.bfloat16)[None]
    return (byte_grad, main_grad)


def solution(mesh):
    return jax.shard_map(
        shards,
        mesh=mesh,
        in_specs=(
            P(("groups", "pipe"), "seq", "tensor"),
            P(("groups", "pipe"), "seq", "tensor"),
            P(("groups", "pipe"), "seq", "tensor"),
            P(("groups", "pipe"), "seq", "tensor"),
            P(("groups", "pipe"), "seq", "tensor"),
            P(("groups", "pipe"), None),
            P("seq", "tensor"),
            P("seq", "tensor"),
        ),
        out_specs=(P(("groups", "pipe"), "seq", "tensor"), P(("groups", "pipe"), "seq", "tensor")),
        check_vma=False,
    )
```

```python
import jax
import jax.numpy as jnp
from jax import lax
from jax.experimental import pallas as pl
from jax.experimental.pallas import tpu as pltpu
from jax.sharding import PartitionSpec as P

epsilon = 1e-06


def passed_along(x, axis, by):
    length = lax.axis_size(axis)
    pairs = [(i, i + by) for i in range(length) if 0 <= i + by < length]
    return lax.ppermute(x, axis, pairs)


reach = 2


def swapped(x, axis):
    length = lax.axis_size(axis)
    return lax.ppermute(x, axis, [(i, length - 1 - i) for i in range(length)])


def passed_on(x, axis, by, came_from):
    length = lax.axis_size(axis)
    pairs = [
        (i, i + by) for i in range(length) if 0 <= i + by < length and 0 <= i + came_from < length
    ]
    return lax.ppermute(x, axis, pairs)


def second_neighbours(right, left):
    return passed_on(right, "seq", 1, -1), passed_on(left, "seq", -1, 1)


def after(value, *others):
    def kernel(*refs):
        del refs

    anywhere = pl.BlockSpec(memory_space=pl.ANY)
    return pl.pallas_call(
        kernel,
        out_shape=jax.ShapeDtypeStruct(value.shape, value.dtype),
        in_specs=[anywhere] * (1 + len(others)),
        out_specs=anywhere,
        input_output_aliases={0: 0},
        name="after",
    )(value, *others)


def byte_sums_kernel(shard_ref, bounds_ref, cotangent_ref, query_ref, key_ref, *refs):
    blocks, out_ref = refs[:-1], refs[-1]
    rows, width = query_ref.shape
    span_rows = blocks[reach].shape[0]
    shard = shard_ref[0]
    row = lax.broadcasted_iota(jnp.int32, (rows, 1), 0)
    held = (bounds_ref[...] <= shard * rows + row).astype(jnp.float32)
    span_of = jnp.sum(held, 1, keepdims=True).astype(jnp.int32) - 1
    place = span_of - (shard - reach) * span_rows
    column = lax.broadcasted_iota(jnp.int32, (rows, span_rows), 1)
    pickers = [
        (place - i * span_rows == column).astype(jnp.float32).astype(jnp.bfloat16)
        for i in range(len(blocks))
    ]
    last_row = blocks[reach - 1].shape[0] - 1
    tile = 384
    totals = [jnp.zeros((rows, 128), jnp.float32)] * 4
    for start in range(0, width, tile):
        cols = pl.ds(start, tile)
        upsampled = jnp.zeros((rows, tile), jnp.float32)
        for picker, block in zip(pickers, blocks):
            upsampled = upsampled + jnp.dot(
                picker, block[:span_rows, cols], preferred_element_type=jnp.float32
            )
        query = query_ref[:, cols].astype(jnp.float32)
        previous = pltpu.roll(key_ref[:, cols].astype(jnp.float32), 1, 0)
        edge = blocks[reach - 1][last_row - 15 :, cols].astype(jnp.float32)[15:16]
        previous = jnp.where(row == 0, edge, previous)
        cotangent = cotangent_ref[:, cols].astype(jnp.float32)
        terms = [query * previous, query * query, previous * previous, cotangent * upsampled]
        for piece in range(0, tile, 128):
            totals = [
                total + term[:, piece : piece + 128] for total, term in zip(totals, terms)
            ]
    lines = [jnp.sum(total.T, 0, keepdims=True) for total in totals]
    out_ref[...] = jnp.concatenate(lines + [jnp.zeros((4, rows), jnp.float32)], 0)


def byte_sums(shard_index, bounds, cotangent, query_rows, key_rows, blocks):
    rows = query_rows.shape[0]
    vmem = pl.BlockSpec(memory_space=pltpu.VMEM)
    return pl.pallas_call(
        byte_sums_kernel,
        out_shape=jax.ShapeDtypeStruct((8, rows), jnp.float32),
        in_specs=[pl.BlockSpec(memory_space=pltpu.SMEM)] + [vmem] * (4 + len(blocks)),
        out_specs=vmem,
        compiler_params=pltpu.CompilerParams(vmem_limit_bytes=40 * 1024 * 1024),
        name="byte_sums",
    )(shard_index[None], bounds, cotangent, query_rows, key_rows, *blocks)


def product(rows, weight):
    return lax.dot_general(
        rows, weight, (((1,), (1,)), ((), ())), preferred_element_type=jnp.float32
    )


def shards(out_grad, queries, keys, main_out, main_in_grad, boundaries, query_weight, key_weight):
    cotangent = out_grad[0]
    query_rows = queries[0]
    key_rows = keys[0]
    bounds_row = boundaries[0]
    row_count = cotangent.shape[0]
    span_rows = main_out.shape[1]
    shard_index = lax.axis_index("seq")
    seq_count = lax.axis_size("seq")
    tensor_count = lax.axis_size("tensor")
    tensor_index = lax.axis_index("tensor")
    group_index = lax.axis_index("groups")
    pipe_index = lax.axis_index("pipe")
    group_rows = query_weight.shape[0] // lax.axis_size("groups")
    half_cols = query_weight.shape[1] // lax.axis_size("pipe")

    def columns(x, index):
        return lax.dynamic_slice_in_dim(x, index * half_cols, half_cols, 1)

    first_rows = group_rows * 2 // 3 // 16 * 16
    cuts = [(0, first_rows), (first_rows, group_rows)]
    out_right = passed_along(jnp.concatenate([main_out[0], key_rows[-16:]], 0), "seq", 1)
    out_left = passed_along(jnp.concatenate([main_out[0], query_rows[:16]], 0), "seq", -1)
    query_other = swapped(query_rows, "groups")
    key_other = swapped(key_rows, "groups")
    own_weights = []
    for low, high in cuts:
        piece = jnp.concatenate(
            [
                lax.dynamic_slice(
                    weight,
                    (group_index * group_rows + low, pipe_index * half_cols),
                    (high - low, half_cols),
                )
                for weight in (query_weight, key_weight)
            ],
            1,
        )
        if own_weights:
            piece = after(piece, out_right)
        own_weights.append(lax.all_gather(piece, "seq", axis=0, tiled=True))
    out_far_right, out_far_left = second_neighbours(out_right, out_left)
    last_key, next_query = out_right[-1:], out_left[span_rows : span_rows + 1]
    edges_other = swapped(jnp.concatenate([last_key, next_query], 0), "groups")
    last_key_other, next_query_other = edges_other[:1], edges_other[1:]
    blocks = [out_far_right, out_right, main_out[0], out_left, out_far_left]
    sums = byte_sums(shard_index, boundaries, cotangent, query_rows, key_rows, blocks)

    positions = shard_index * row_count + jnp.arange(row_count, dtype=jnp.int32)
    span_of = jnp.sum((bounds_row[None, :] <= positions[:, None]).astype(jnp.int32), 1) - 1
    starts = jnp.any(bounds_row[None, :] == positions[:, None], 1)
    place = span_of - (shard_index - reach) * span_rows
    window_rows = (2 * reach + 1) * span_rows
    selector = place[:, None] == jnp.arange(window_rows, dtype=jnp.int32)[None, :]
    cotangent_wide = cotangent.astype(jnp.float32)
    if tensor_count == 2:
        sums = sums + swapped(sums, "tensor")
    else:
        sums = lax.psum(sums, "tensor")
    cross_sum, query_sum, key_sum, conf_grad = sums[:4]
    query_scale = lax.rsqrt(query_sum + epsilon)
    key_scale = lax.rsqrt(key_sum + epsilon)
    cosine = cross_sum * query_scale * key_scale
    probability = jnp.where(positions == 0, 1.0, 0.5 * (1.0 - cosine))
    confidence = jnp.where(starts, probability, 1.0 - probability)
    sign = jnp.where(starts, 1.0, -1.0)
    cos_grad = jnp.where(positions == 0, 0.0, -0.5 * sign * conf_grad)
    factors = jnp.stack(
        [
            cos_grad * (query_scale * key_scale),
            cos_grad * (cosine * query_scale * query_scale),
            cos_grad * (cosine * key_scale * key_scale),
        ]
    )
    next_factors = passed_along(factors[:, :1], "seq", -1)
    factors = jnp.concatenate([factors, next_factors], 1)
    factors_other = swapped(factors, "groups")

    def grads(queries_here, keys_here, key_before, query_after, here, index):
        previous = jnp.concatenate([columns(key_before, index), columns(keys_here, index)[:-1]], 0)
        current = columns(queries_here, index)
        following = jnp.concatenate([current[1:], columns(query_after, index)], 0)
        ahead, here = here[:, 1:], here[:, :-1]
        query_grad = here[0][:, None] * previous.astype(jnp.float32)
        query_grad = query_grad - here[1][:, None] * current.astype(jnp.float32)
        key_grad = ahead[0][:, None] * following.astype(jnp.float32)
        key_grad = key_grad - ahead[2][:, None] * columns(keys_here, index).astype(jnp.float32)
        return jnp.concatenate([query_grad.astype(jnp.bfloat16), key_grad.astype(jnp.bfloat16)], 1)

    def both_grads(index):
        own = grads(query_rows, key_rows, last_key, next_query, factors, index)
        other = grads(
            query_other,
            key_other,
            last_key_other,
            next_query_other,
            factors_other,
            index,
        )
        return jnp.concatenate([own, other], 0)

    own_side, other_side = both_grads(pipe_index), both_grads(1 - pipe_index)

    def span_part(ready):
        conf_high = confidence.astype(jnp.bfloat16)
        conf_low = (confidence - conf_high.astype(jnp.float32)).astype(jnp.bfloat16)
        zero_weight = jnp.zeros((), jnp.bfloat16)
        weight_high = jnp.where(selector, conf_high[:, None], zero_weight)
        weight_low = jnp.where(selector, conf_low[:, None], zero_weight)
        contract = (((0,), (0,)), ((), ()))
        span_terms = lax.dot_general(
            weight_high, cotangent, contract, preferred_element_type=jnp.float32
        )
        span_terms = span_terms + lax.dot_general(
            weight_low, cotangent, contract, preferred_element_type=jnp.float32
        )
        terms = [span_terms[i * span_rows : (i + 1) * span_rows] for i in range(2 * reach + 1)]

        parts = after(jnp.concatenate(terms, 0).astype(jnp.bfloat16), ready)
        received = [
            passed_along(parts[i * span_rows : (i + 1) * span_rows], "seq", i - reach)
            for i in range(2 * reach + 1)
            if i != reach
        ]
        return terms[reach], received

    window_grad = lax.all_gather(
        after(main_in_grad[0], own_weights[0]), "seq", axis=0, tiled=True
    )
    span_index = jnp.arange(window_grad.shape[0], dtype=jnp.int32)
    start_picker = ((span_of[:, None] == span_index[None, :]) & starts[:, None]).astype(jnp.bfloat16)
    start_grad = jnp.dot(start_picker, window_grad, preferred_element_type=jnp.float32)

    def partial(own_weight, other_weight):
        total = product(own_side, own_weight) + product(other_side, other_weight)
        return total.astype(jnp.bfloat16)

    pieces = []
    span_sums, received = span_part(factors_other)
    far_part = None
    for own_weight in own_weights:
        if far_part is not None:
            own_weight = after(own_weight, far_part)
        other_weight = swapped(own_weight, "pipe")
        block_rows = own_weight.shape[0] // tensor_count
        if tensor_count == 2:

            def half(index):
                return [
                    lax.dynamic_slice_in_dim(weight, index * block_rows, block_rows, 0)
                    for weight in (own_weight, other_weight)
                ]

            far_part = partial(*half(1 - tensor_index))
            incoming = swapped(far_part, "tensor").astype(jnp.float32)
            total = partial(*half(tensor_index)).astype(jnp.float32) + incoming
        else:
            far_part = partial(own_weight, other_weight)
            total = lax.psum_scatter(
                far_part, "tensor", scatter_dimension=1, tiled=True
            ).astype(jnp.float32)
        own = total[:row_count]
        returned = total[row_count:].astype(jnp.bfloat16)
        arrived = swapped(returned, "groups").astype(jnp.float32)
        pieces.append(
            [jnp.where(group_index == 0, own, arrived), jnp.where(group_index == 0, arrived, own)]
        )
    span_sums = after(span_sums, far_part)
    for block in received:
        span_sums = span_sums + block.astype(jnp.float32)
    main_grad = span_sums.astype(jnp.bfloat16)[None]
    widths = [high - low for low, high in cuts]
    routing = jnp.concatenate(
        [
            piece[group][:, s * width : (s + 1) * width]
            for s in range(seq_count // tensor_count)
            for group in range(2)
            for piece, width in zip(pieces, widths)
        ],
        1,
    )
    byte_grad = (cotangent_wide + start_grad + routing).astype(jnp.bfloat16)[None]
    return (byte_grad, main_grad)


def solution(mesh):
    return jax.shard_map(
        shards,
        mesh=mesh,
        in_specs=(
            P(("groups", "pipe"), "seq", "tensor"),
            P(("groups", "pipe"), "seq", "tensor"),
            P(("groups", "pipe"), "seq", "tensor"),
            P(("groups", "pipe"), "seq", "tensor"),
            P(("groups", "pipe"), "seq", "tensor"),
            P(("groups", "pipe"), None),
            P("seq", "tensor"),
            P("seq", "tensor"),
        ),
        out_specs=(P(("groups", "pipe"), "seq", "tensor"), P(("groups", "pipe"), "seq", "tensor")),
        check_vma=False,
    )
```

```python
import jax
import jax.numpy as jnp
from jax import lax
from jax.experimental import pallas as pl
from jax.experimental.pallas import tpu as pltpu
from jax.sharding import PartitionSpec as P

epsilon = 1e-06


def passed_along(x, axis, by):
    length = lax.axis_size(axis)
    pairs = [(i, i + by) for i in range(length) if 0 <= i + by < length]
    return lax.ppermute(x, axis, pairs)


reach = 2


def swapped(x, axis):
    length = lax.axis_size(axis)
    return lax.ppermute(x, axis, [(i, length - 1 - i) for i in range(length)])


def passed_on(x, axis, by, came_from):
    length = lax.axis_size(axis)
    pairs = [
        (i, i + by) for i in range(length) if 0 <= i + by < length and 0 <= i + came_from < length
    ]
    return lax.ppermute(x, axis, pairs)


def second_neighbours(right, left):
    return passed_on(right, "seq", 1, -1), passed_on(left, "seq", -1, 1)


def after(value, *others):
    def kernel(*refs):
        del refs

    anywhere = pl.BlockSpec(memory_space=pl.ANY)
    return pl.pallas_call(
        kernel,
        out_shape=jax.ShapeDtypeStruct(value.shape, value.dtype),
        in_specs=[anywhere] * (1 + len(others)),
        out_specs=anywhere,
        input_output_aliases={0: 0},
        name="after",
    )(value, *others)


def byte_sums_kernel(shard_ref, bounds_ref, cotangent_ref, query_ref, key_ref, *refs):
    blocks, out_ref = refs[:-1], refs[-1]
    rows, width = query_ref.shape
    span_rows = blocks[reach].shape[0]
    shard = shard_ref[0]
    row = lax.broadcasted_iota(jnp.int32, (rows, 1), 0)
    held = (bounds_ref[...] <= shard * rows + row).astype(jnp.float32)
    span_of = jnp.sum(held, 1, keepdims=True).astype(jnp.int32) - 1
    place = span_of - (shard - reach) * span_rows
    column = lax.broadcasted_iota(jnp.int32, (rows, span_rows), 1)
    pickers = [
        (place - i * span_rows == column).astype(jnp.float32).astype(jnp.bfloat16)
        for i in range(len(blocks))
    ]
    last_row = blocks[reach - 1].shape[0] - 1
    tile = 384
    totals = [jnp.zeros((rows, 128), jnp.float32)] * 4
    for start in range(0, width, tile):
        cols = pl.ds(start, tile)
        upsampled = jnp.zeros((rows, tile), jnp.float32)
        for picker, block in zip(pickers, blocks):
            upsampled = upsampled + jnp.dot(
                picker, block[:span_rows, cols], preferred_element_type=jnp.float32
            )
        query = query_ref[:, cols].astype(jnp.float32)
        previous = pltpu.roll(key_ref[:, cols].astype(jnp.float32), 1, 0)
        edge = blocks[reach - 1][last_row - 15 :, cols].astype(jnp.float32)[15:16]
        previous = jnp.where(row == 0, edge, previous)
        cotangent = cotangent_ref[:, cols].astype(jnp.float32)
        terms = [query * previous, query * query, previous * previous, cotangent * upsampled]
        for piece in range(0, tile, 128):
            totals = [
                total + term[:, piece : piece + 128] for total, term in zip(totals, terms)
            ]
    lines = [jnp.sum(total.T, 0, keepdims=True) for total in totals]
    out_ref[...] = jnp.concatenate(lines + [jnp.zeros((4, rows), jnp.float32)], 0)


def byte_sums(shard_index, bounds, cotangent, query_rows, key_rows, blocks):
    rows = query_rows.shape[0]
    vmem = pl.BlockSpec(memory_space=pltpu.VMEM)
    return pl.pallas_call(
        byte_sums_kernel,
        out_shape=jax.ShapeDtypeStruct((8, rows), jnp.float32),
        in_specs=[pl.BlockSpec(memory_space=pltpu.SMEM)] + [vmem] * (4 + len(blocks)),
        out_specs=vmem,
        compiler_params=pltpu.CompilerParams(vmem_limit_bytes=40 * 1024 * 1024),
        name="byte_sums",
    )(shard_index[None], bounds, cotangent, query_rows, key_rows, *blocks)


def product(rows, weight):
    return lax.dot_general(
        rows, weight, (((1,), (1,)), ((), ())), preferred_element_type=jnp.float32
    )


def shards(out_grad, queries, keys, main_out, main_in_grad, boundaries, query_weight, key_weight):
    cotangent = out_grad[0]
    query_rows = queries[0]
    key_rows = keys[0]
    bounds_row = boundaries[0]
    row_count = cotangent.shape[0]
    span_rows = main_out.shape[1]
    shard_index = lax.axis_index("seq")
    seq_count = lax.axis_size("seq")
    tensor_count = lax.axis_size("tensor")
    tensor_index = lax.axis_index("tensor")
    group_index = lax.axis_index("groups")
    pipe_index = lax.axis_index("pipe")
    group_rows = query_weight.shape[0] // lax.axis_size("groups")
    half_cols = query_weight.shape[1] // lax.axis_size("pipe")

    def columns(x, index):
        return lax.dynamic_slice_in_dim(x, index * half_cols, half_cols, 1)

    first_rows = group_rows * 2 // 3 // 16 * 16
    cuts = [(0, first_rows), (first_rows, group_rows)]
    out_right = passed_along(jnp.concatenate([main_out[0], key_rows[-16:]], 0), "seq", 1)
    out_left = passed_along(jnp.concatenate([main_out[0], query_rows[:16]], 0), "seq", -1)
    query_other = swapped(query_rows, "groups")
    key_other = swapped(key_rows, "groups")
    own_weights = []
    for low, high in cuts:
        piece = jnp.concatenate(
            [
                lax.dynamic_slice(
                    weight,
                    (group_index * group_rows + low, pipe_index * half_cols),
                    (high - low, half_cols),
                )
                for weight in (query_weight, key_weight)
            ],
            1,
        )
        if own_weights:
            piece = after(piece, out_right)
        own_weights.append(lax.all_gather(piece, "seq", axis=0, tiled=True))
    out_far_right, out_far_left = second_neighbours(out_right, out_left)
    last_key, next_query = out_right[-1:], out_left[span_rows : span_rows + 1]
    edges_other = swapped(jnp.concatenate([last_key, next_query], 0), "groups")
    last_key_other, next_query_other = edges_other[:1], edges_other[1:]
    blocks = [out_far_right, out_right, main_out[0], out_left, out_far_left]
    sums = byte_sums(shard_index, boundaries, cotangent, query_rows, key_rows, blocks)

    positions = shard_index * row_count + jnp.arange(row_count, dtype=jnp.int32)
    span_of = jnp.sum((bounds_row[None, :] <= positions[:, None]).astype(jnp.int32), 1) - 1
    starts = jnp.any(bounds_row[None, :] == positions[:, None], 1)
    place = span_of - (shard_index - reach) * span_rows
    window_rows = (2 * reach + 1) * span_rows
    selector = place[:, None] == jnp.arange(window_rows, dtype=jnp.int32)[None, :]
    cotangent_wide = cotangent.astype(jnp.float32)
    if tensor_count == 2:
        sums = sums + swapped(sums, "tensor")
    else:
        sums = lax.psum(sums, "tensor")
    cross_sum, query_sum, key_sum, conf_grad = sums[:4]
    query_scale = lax.rsqrt(query_sum + epsilon)
    key_scale = lax.rsqrt(key_sum + epsilon)
    cosine = cross_sum * query_scale * key_scale
    probability = jnp.where(positions == 0, 1.0, 0.5 * (1.0 - cosine))
    confidence = jnp.where(starts, probability, 1.0 - probability)
    sign = jnp.where(starts, 1.0, -1.0)
    cos_grad = jnp.where(positions == 0, 0.0, -0.5 * sign * conf_grad)
    factors = jnp.stack(
        [
            cos_grad * (query_scale * key_scale),
            cos_grad * (cosine * query_scale * query_scale),
            cos_grad * (cosine * key_scale * key_scale),
        ]
    )
    next_factors = passed_along(factors[:, :1], "seq", -1)
    factors = jnp.concatenate([factors, next_factors], 1)
    factors_other = swapped(factors, "groups")

    def grads(queries_here, keys_here, key_before, query_after, here, index):
        previous = jnp.concatenate([columns(key_before, index), columns(keys_here, index)[:-1]], 0)
        current = columns(queries_here, index)
        following = jnp.concatenate([current[1:], columns(query_after, index)], 0)
        ahead, here = here[:, 1:], here[:, :-1]
        query_grad = here[0][:, None] * previous.astype(jnp.float32)
        query_grad = query_grad - here[1][:, None] * current.astype(jnp.float32)
        key_grad = ahead[0][:, None] * following.astype(jnp.float32)
        key_grad = key_grad - ahead[2][:, None] * columns(keys_here, index).astype(jnp.float32)
        return jnp.concatenate([query_grad.astype(jnp.bfloat16), key_grad.astype(jnp.bfloat16)], 1)

    def both_grads(index):
        own = grads(query_rows, key_rows, last_key, next_query, factors, index)
        other = grads(
            query_other,
            key_other,
            last_key_other,
            next_query_other,
            factors_other,
            index,
        )
        return jnp.concatenate([own, other], 0)

    own_side, other_side = both_grads(pipe_index), both_grads(1 - pipe_index)

    def span_part(ready):
        conf_high = confidence.astype(jnp.bfloat16)
        conf_low = (confidence - conf_high.astype(jnp.float32)).astype(jnp.bfloat16)
        zero_weight = jnp.zeros((), jnp.bfloat16)
        weight_high = jnp.where(selector, conf_high[:, None], zero_weight)
        weight_low = jnp.where(selector, conf_low[:, None], zero_weight)
        contract = (((0,), (0,)), ((), ()))
        span_terms = lax.dot_general(
            weight_high, cotangent, contract, preferred_element_type=jnp.float32
        )
        span_terms = span_terms + lax.dot_general(
            weight_low, cotangent, contract, preferred_element_type=jnp.float32
        )
        terms = [span_terms[i * span_rows : (i + 1) * span_rows] for i in range(2 * reach + 1)]

        parts = after(jnp.concatenate(terms, 0).astype(jnp.bfloat16), ready)
        received = [
            passed_along(parts[i * span_rows : (i + 1) * span_rows], "seq", i - reach)
            for i in range(2 * reach + 1)
            if i != reach
        ]
        return terms[reach], received

    window_grad = lax.all_gather(
        after(main_in_grad[0], own_weights[0]), "seq", axis=0, tiled=True
    )
    span_index = jnp.arange(window_grad.shape[0], dtype=jnp.int32)
    start_picker = ((span_of[:, None] == span_index[None, :]) & starts[:, None]).astype(jnp.bfloat16)
    start_grad = jnp.dot(start_picker, window_grad, preferred_element_type=jnp.float32)

    def partial(own_weight, other_weight):
        total = product(own_side, own_weight) + product(other_side, other_weight)
        return total.astype(jnp.bfloat16)

    pieces = []
    span_sums, received = span_part(factors_other)
    far_part = None
    for own_weight in own_weights:
        if far_part is not None:
            own_weight = after(own_weight, far_part)
        other_weight = swapped(own_weight, "pipe")
        block_rows = own_weight.shape[0] // tensor_count
        if tensor_count == 2:

            def half(index):
                return [
                    lax.dynamic_slice_in_dim(weight, index * block_rows, block_rows, 0)
                    for weight in (own_weight, other_weight)
                ]

            far_part = partial(*half(1 - tensor_index))
            incoming = swapped(far_part, "tensor").astype(jnp.float32)
            total = partial(*half(tensor_index)).astype(jnp.float32) + incoming
        else:
            far_part = partial(own_weight, other_weight)
            total = lax.psum_scatter(
                far_part, "tensor", scatter_dimension=1, tiled=True
            ).astype(jnp.float32)
        own = total[:row_count]
        returned = total[row_count:].astype(jnp.bfloat16)
        if not pieces:
            returned = after(returned, *received)
        arrived = swapped(returned, "groups").astype(jnp.float32)
        pieces.append(
            [jnp.where(group_index == 0, own, arrived), jnp.where(group_index == 0, arrived, own)]
        )
    span_sums = after(span_sums, far_part)
    for block in received:
        span_sums = span_sums + block.astype(jnp.float32)
    main_grad = span_sums.astype(jnp.bfloat16)[None]
    widths = [high - low for low, high in cuts]
    routing = jnp.concatenate(
        [
            piece[group][:, s * width : (s + 1) * width]
            for s in range(seq_count // tensor_count)
            for group in range(2)
            for piece, width in zip(pieces, widths)
        ],
        1,
    )
    byte_grad = (cotangent_wide + start_grad + routing).astype(jnp.bfloat16)[None]
    return (byte_grad, main_grad)


def solution(mesh):
    return jax.shard_map(
        shards,
        mesh=mesh,
        in_specs=(
            P(("groups", "pipe"), "seq", "tensor"),
            P(("groups", "pipe"), "seq", "tensor"),
            P(("groups", "pipe"), "seq", "tensor"),
            P(("groups", "pipe"), "seq", "tensor"),
            P(("groups", "pipe"), "seq", "tensor"),
            P(("groups", "pipe"), None),
            P("seq", "tensor"),
            P("seq", "tensor"),
        ),
        out_specs=(P(("groups", "pipe"), "seq", "tensor"), P(("groups", "pipe"), "seq", "tensor")),
        check_vma=False,
    )
```

```python
import jax
import jax.numpy as jnp
from jax import lax
from jax.experimental import pallas as pl
from jax.experimental.pallas import tpu as pltpu
from jax.sharding import PartitionSpec as P

epsilon = 1e-06


def passed_along(x, axis, by):
    length = lax.axis_size(axis)
    pairs = [(i, i + by) for i in range(length) if 0 <= i + by < length]
    return lax.ppermute(x, axis, pairs)


reach = 2


def swapped(x, axis):
    length = lax.axis_size(axis)
    return lax.ppermute(x, axis, [(i, length - 1 - i) for i in range(length)])


def passed_on(x, axis, by, came_from):
    length = lax.axis_size(axis)
    pairs = [
        (i, i + by) for i in range(length) if 0 <= i + by < length and 0 <= i + came_from < length
    ]
    return lax.ppermute(x, axis, pairs)


def second_neighbours(right, left):
    return passed_on(right, "seq", 1, -1), passed_on(left, "seq", -1, 1)


def after(value, *others):
    def kernel(*refs):
        del refs

    anywhere = pl.BlockSpec(memory_space=pl.ANY)
    return pl.pallas_call(
        kernel,
        out_shape=jax.ShapeDtypeStruct(value.shape, value.dtype),
        in_specs=[anywhere] * (1 + len(others)),
        out_specs=anywhere,
        input_output_aliases={0: 0},
        name="after",
    )(value, *others)


def byte_sums_kernel(shard_ref, bounds_ref, cotangent_ref, query_ref, key_ref, *refs):
    blocks, out_ref = refs[:-1], refs[-1]
    rows, width = query_ref.shape
    span_rows = blocks[reach].shape[0]
    shard = shard_ref[0]
    row = lax.broadcasted_iota(jnp.int32, (rows, 1), 0)
    held = (bounds_ref[...] <= shard * rows + row).astype(jnp.float32)
    span_of = jnp.sum(held, 1, keepdims=True).astype(jnp.int32) - 1
    place = span_of - (shard - reach) * span_rows
    column = lax.broadcasted_iota(jnp.int32, (rows, span_rows), 1)
    pickers = [
        (place - i * span_rows == column).astype(jnp.float32).astype(jnp.bfloat16)
        for i in range(len(blocks))
    ]
    last_row = blocks[reach - 1].shape[0] - 1
    tile = 384
    totals = [jnp.zeros((rows, 128), jnp.float32)] * 4
    for start in range(0, width, tile):
        cols = pl.ds(start, tile)
        upsampled = jnp.zeros((rows, tile), jnp.float32)
        for picker, block in zip(pickers, blocks):
            upsampled = upsampled + jnp.dot(
                picker, block[:span_rows, cols], preferred_element_type=jnp.float32
            )
        query = query_ref[:, cols].astype(jnp.float32)
        previous = pltpu.roll(key_ref[:, cols].astype(jnp.float32), 1, 0)
        edge = blocks[reach - 1][last_row - 15 :, cols].astype(jnp.float32)[15:16]
        previous = jnp.where(row == 0, edge, previous)
        cotangent = cotangent_ref[:, cols].astype(jnp.float32)
        terms = [query * previous, query * query, previous * previous, cotangent * upsampled]
        for piece in range(0, tile, 128):
            totals = [
                total + term[:, piece : piece + 128] for total, term in zip(totals, terms)
            ]
    lines = [jnp.sum(total.T, 0, keepdims=True) for total in totals]
    out_ref[...] = jnp.concatenate(lines + [jnp.zeros((4, rows), jnp.float32)], 0)


def byte_sums(shard_index, bounds, cotangent, query_rows, key_rows, blocks):
    rows = query_rows.shape[0]
    vmem = pl.BlockSpec(memory_space=pltpu.VMEM)
    return pl.pallas_call(
        byte_sums_kernel,
        out_shape=jax.ShapeDtypeStruct((8, rows), jnp.float32),
        in_specs=[pl.BlockSpec(memory_space=pltpu.SMEM)] + [vmem] * (4 + len(blocks)),
        out_specs=vmem,
        compiler_params=pltpu.CompilerParams(vmem_limit_bytes=40 * 1024 * 1024),
        name="byte_sums",
    )(shard_index[None], bounds, cotangent, query_rows, key_rows, *blocks)


def product(rows, weight):
    return lax.dot_general(
        rows, weight, (((1,), (1,)), ((), ())), preferred_element_type=jnp.float32
    )


def shards(out_grad, queries, keys, main_out, main_in_grad, boundaries, query_weight, key_weight):
    cotangent = out_grad[0]
    query_rows = queries[0]
    key_rows = keys[0]
    bounds_row = boundaries[0]
    row_count = cotangent.shape[0]
    span_rows = main_out.shape[1]
    shard_index = lax.axis_index("seq")
    seq_count = lax.axis_size("seq")
    tensor_count = lax.axis_size("tensor")
    tensor_index = lax.axis_index("tensor")
    group_index = lax.axis_index("groups")
    pipe_index = lax.axis_index("pipe")
    group_rows = query_weight.shape[0] // lax.axis_size("groups")
    half_cols = query_weight.shape[1] // lax.axis_size("pipe")

    def columns(x, index):
        return lax.dynamic_slice_in_dim(x, index * half_cols, half_cols, 1)

    first_rows = group_rows * 2 // 3 // 16 * 16
    cuts = [(0, first_rows), (first_rows, group_rows)]
    out_right = passed_along(jnp.concatenate([main_out[0], key_rows[-16:]], 0), "seq", 1)
    out_left = passed_along(jnp.concatenate([main_out[0], query_rows[:16]], 0), "seq", -1)
    query_other = swapped(query_rows, "groups")
    key_other = swapped(key_rows, "groups")
    own_weights = []
    for low, high in cuts:
        piece = jnp.concatenate(
            [
                lax.dynamic_slice(
                    weight,
                    (group_index * group_rows + low, pipe_index * half_cols),
                    (high - low, half_cols),
                )
                for weight in (query_weight, key_weight)
            ],
            1,
        )
        if own_weights:
            piece = after(piece, out_right)
        own_weights.append(lax.all_gather(piece, "seq", axis=0, tiled=True))
    out_far_right, out_far_left = second_neighbours(out_right, out_left)
    last_key, next_query = out_right[-1:], out_left[span_rows : span_rows + 1]
    edges_other = swapped(jnp.concatenate([last_key, next_query], 0), "groups")
    last_key_other, next_query_other = edges_other[:1], edges_other[1:]
    blocks = [out_far_right, out_right, main_out[0], out_left, out_far_left]
    sums = byte_sums(shard_index, boundaries, cotangent, query_rows, key_rows, blocks)

    positions = shard_index * row_count + jnp.arange(row_count, dtype=jnp.int32)
    span_of = jnp.sum((bounds_row[None, :] <= positions[:, None]).astype(jnp.int32), 1) - 1
    starts = jnp.any(bounds_row[None, :] == positions[:, None], 1)
    place = span_of - (shard_index - reach) * span_rows
    window_rows = (2 * reach + 1) * span_rows
    selector = place[:, None] == jnp.arange(window_rows, dtype=jnp.int32)[None, :]
    cotangent_wide = cotangent.astype(jnp.float32)
    if tensor_count == 2:
        sums = sums + swapped(sums, "tensor")
    else:
        sums = lax.psum(sums, "tensor")
    cross_sum, query_sum, key_sum, conf_grad = sums[:4]
    query_scale = lax.rsqrt(query_sum + epsilon)
    key_scale = lax.rsqrt(key_sum + epsilon)
    cosine = cross_sum * query_scale * key_scale
    probability = jnp.where(positions == 0, 1.0, 0.5 * (1.0 - cosine))
    confidence = jnp.where(starts, probability, 1.0 - probability)
    sign = jnp.where(starts, 1.0, -1.0)
    cos_grad = jnp.where(positions == 0, 0.0, -0.5 * sign * conf_grad)
    factors = jnp.stack(
        [
            cos_grad * (query_scale * key_scale),
            cos_grad * (cosine * query_scale * query_scale),
            cos_grad * (cosine * key_scale * key_scale),
        ]
    )
    next_factors = passed_along(factors[:, :1], "seq", -1)
    factors = jnp.concatenate([factors, next_factors], 1)
    factors_other = swapped(factors, "groups")

    def grads(queries_here, keys_here, key_before, query_after, here, index):
        previous = jnp.concatenate([columns(key_before, index), columns(keys_here, index)[:-1]], 0)
        current = columns(queries_here, index)
        following = jnp.concatenate([current[1:], columns(query_after, index)], 0)
        ahead, here = here[:, 1:], here[:, :-1]
        query_grad = here[0][:, None] * previous.astype(jnp.float32)
        query_grad = query_grad - here[1][:, None] * current.astype(jnp.float32)
        key_grad = ahead[0][:, None] * following.astype(jnp.float32)
        key_grad = key_grad - ahead[2][:, None] * columns(keys_here, index).astype(jnp.float32)
        return jnp.concatenate([query_grad.astype(jnp.bfloat16), key_grad.astype(jnp.bfloat16)], 1)

    def both_grads(index):
        own = grads(query_rows, key_rows, last_key, next_query, factors, index)
        other = grads(
            query_other,
            key_other,
            last_key_other,
            next_query_other,
            factors_other,
            index,
        )
        return jnp.concatenate([own, other], 0)

    own_side, other_side = both_grads(pipe_index), both_grads(1 - pipe_index)

    def span_part(ready):
        conf_high = confidence.astype(jnp.bfloat16)
        conf_low = (confidence - conf_high.astype(jnp.float32)).astype(jnp.bfloat16)
        zero_weight = jnp.zeros((), jnp.bfloat16)
        weight_high = jnp.where(selector, conf_high[:, None], zero_weight)
        weight_low = jnp.where(selector, conf_low[:, None], zero_weight)
        contract = (((0,), (0,)), ((), ()))
        span_terms = lax.dot_general(
            weight_high, cotangent, contract, preferred_element_type=jnp.float32
        )
        span_terms = span_terms + lax.dot_general(
            weight_low, cotangent, contract, preferred_element_type=jnp.float32
        )
        terms = [span_terms[i * span_rows : (i + 1) * span_rows] for i in range(2 * reach + 1)]

        parts = after(jnp.concatenate(terms, 0).astype(jnp.bfloat16), ready)
        received = [
            passed_along(parts[i * span_rows : (i + 1) * span_rows], "seq", i - reach)
            for i in range(2 * reach + 1)
            if i != reach
        ]
        return terms[reach], received

    window_grad = lax.all_gather(
        after(main_in_grad[0], own_weights[0]), "seq", axis=0, tiled=True
    )
    span_index = jnp.arange(window_grad.shape[0], dtype=jnp.int32)
    start_picker = ((span_of[:, None] == span_index[None, :]) & starts[:, None]).astype(jnp.bfloat16)
    start_grad = jnp.dot(start_picker, window_grad, preferred_element_type=jnp.float32)

    def partial(own_weight, other_weight):
        total = product(own_side, own_weight) + product(other_side, other_weight)
        return total.astype(jnp.bfloat16)

    pieces = []
    span_sums, received = span_part(factors_other)
    far_part = None
    for own_weight in own_weights:
        if far_part is not None:
            own_weight = after(own_weight, far_part, *received)
        other_weight = swapped(own_weight, "pipe")
        block_rows = own_weight.shape[0] // tensor_count
        if tensor_count == 2:

            def half(index):
                return [
                    lax.dynamic_slice_in_dim(weight, index * block_rows, block_rows, 0)
                    for weight in (own_weight, other_weight)
                ]

            far_part = partial(*half(1 - tensor_index))
            incoming = swapped(far_part, "tensor").astype(jnp.float32)
            total = partial(*half(tensor_index)).astype(jnp.float32) + incoming
        else:
            far_part = partial(own_weight, other_weight)
            total = lax.psum_scatter(
                far_part, "tensor", scatter_dimension=1, tiled=True
            ).astype(jnp.float32)
        own = total[:row_count]
        returned = total[row_count:].astype(jnp.bfloat16)
        arrived = swapped(returned, "groups").astype(jnp.float32)
        pieces.append(
            [jnp.where(group_index == 0, own, arrived), jnp.where(group_index == 0, arrived, own)]
        )
    span_sums = after(span_sums, far_part)
    for block in received:
        span_sums = span_sums + block.astype(jnp.float32)
    main_grad = span_sums.astype(jnp.bfloat16)[None]
    widths = [high - low for low, high in cuts]
    routing = jnp.concatenate(
        [
            piece[group][:, s * width : (s + 1) * width]
            for s in range(seq_count // tensor_count)
            for group in range(2)
            for piece, width in zip(pieces, widths)
        ],
        1,
    )
    byte_grad = (cotangent_wide + start_grad + routing).astype(jnp.bfloat16)[None]
    return (byte_grad, main_grad)


def solution(mesh):
    return jax.shard_map(
        shards,
        mesh=mesh,
        in_specs=(
            P(("groups", "pipe"), "seq", "tensor"),
            P(("groups", "pipe"), "seq", "tensor"),
            P(("groups", "pipe"), "seq", "tensor"),
            P(("groups", "pipe"), "seq", "tensor"),
            P(("groups", "pipe"), "seq", "tensor"),
            P(("groups", "pipe"), None),
            P("seq", "tensor"),
            P("seq", "tensor"),
        ),
        out_specs=(P(("groups", "pipe"), "seq", "tensor"), P(("groups", "pipe"), "seq", "tensor")),
        check_vma=False,
    )
```

```python
import jax
import jax.numpy as jnp
from jax import lax
from jax.experimental import pallas as pl
from jax.experimental.pallas import tpu as pltpu
from jax.sharding import PartitionSpec as P

epsilon = 1e-06


def passed_along(x, axis, by):
    length = lax.axis_size(axis)
    pairs = [(i, i + by) for i in range(length) if 0 <= i + by < length]
    return lax.ppermute(x, axis, pairs)


reach = 2


def swapped(x, axis):
    length = lax.axis_size(axis)
    return lax.ppermute(x, axis, [(i, length - 1 - i) for i in range(length)])


def passed_on(x, axis, by, came_from):
    length = lax.axis_size(axis)
    pairs = [
        (i, i + by) for i in range(length) if 0 <= i + by < length and 0 <= i + came_from < length
    ]
    return lax.ppermute(x, axis, pairs)


def second_neighbours(right, left):
    return passed_on(right, "seq", 1, -1), passed_on(left, "seq", -1, 1)


def after(value, *others):
    def kernel(*refs):
        del refs

    anywhere = pl.BlockSpec(memory_space=pl.ANY)
    return pl.pallas_call(
        kernel,
        out_shape=jax.ShapeDtypeStruct(value.shape, value.dtype),
        in_specs=[anywhere] * (1 + len(others)),
        out_specs=anywhere,
        input_output_aliases={0: 0},
        name="after",
    )(value, *others)


def byte_sums_kernel(shard_ref, bounds_ref, cotangent_ref, query_ref, key_ref, *refs):
    blocks, out_ref = refs[:-1], refs[-1]
    rows, width = query_ref.shape
    span_rows = blocks[reach].shape[0]
    shard = shard_ref[0]
    row = lax.broadcasted_iota(jnp.int32, (rows, 1), 0)
    held = (bounds_ref[...] <= shard * rows + row).astype(jnp.float32)
    span_of = jnp.sum(held, 1, keepdims=True).astype(jnp.int32) - 1
    place = span_of - (shard - reach) * span_rows
    column = lax.broadcasted_iota(jnp.int32, (rows, span_rows), 1)
    pickers = [
        (place - i * span_rows == column).astype(jnp.float32).astype(jnp.bfloat16)
        for i in range(len(blocks))
    ]
    last_row = blocks[reach - 1].shape[0] - 1
    tile = 384
    totals = [jnp.zeros((rows, 128), jnp.float32)] * 4
    for start in range(0, width, tile):
        cols = pl.ds(start, tile)
        upsampled = jnp.zeros((rows, tile), jnp.float32)
        for picker, block in zip(pickers, blocks):
            upsampled = upsampled + jnp.dot(
                picker, block[:span_rows, cols], preferred_element_type=jnp.float32
            )
        query = query_ref[:, cols].astype(jnp.float32)
        previous = pltpu.roll(key_ref[:, cols].astype(jnp.float32), 1, 0)
        edge = blocks[reach - 1][last_row - 15 :, cols].astype(jnp.float32)[15:16]
        previous = jnp.where(row == 0, edge, previous)
        cotangent = cotangent_ref[:, cols].astype(jnp.float32)
        terms = [query * previous, query * query, previous * previous, cotangent * upsampled]
        for piece in range(0, tile, 128):
            totals = [
                total + term[:, piece : piece + 128] for total, term in zip(totals, terms)
            ]
    lines = [jnp.sum(total.T, 0, keepdims=True) for total in totals]
    out_ref[...] = jnp.concatenate(lines + [jnp.zeros((4, rows), jnp.float32)], 0)


def byte_sums(shard_index, bounds, cotangent, query_rows, key_rows, blocks):
    rows = query_rows.shape[0]
    vmem = pl.BlockSpec(memory_space=pltpu.VMEM)
    return pl.pallas_call(
        byte_sums_kernel,
        out_shape=jax.ShapeDtypeStruct((8, rows), jnp.float32),
        in_specs=[pl.BlockSpec(memory_space=pltpu.SMEM)] + [vmem] * (4 + len(blocks)),
        out_specs=vmem,
        compiler_params=pltpu.CompilerParams(vmem_limit_bytes=40 * 1024 * 1024),
        name="byte_sums",
    )(shard_index[None], bounds, cotangent, query_rows, key_rows, *blocks)


def product(rows, weight):
    return lax.dot_general(
        rows, weight, (((1,), (1,)), ((), ())), preferred_element_type=jnp.float32
    )


def shards(out_grad, queries, keys, main_out, main_in_grad, boundaries, query_weight, key_weight):
    cotangent = out_grad[0]
    query_rows = queries[0]
    key_rows = keys[0]
    bounds_row = boundaries[0]
    row_count = cotangent.shape[0]
    span_rows = main_out.shape[1]
    shard_index = lax.axis_index("seq")
    seq_count = lax.axis_size("seq")
    tensor_count = lax.axis_size("tensor")
    tensor_index = lax.axis_index("tensor")
    group_index = lax.axis_index("groups")
    pipe_index = lax.axis_index("pipe")
    group_rows = query_weight.shape[0] // lax.axis_size("groups")
    half_cols = query_weight.shape[1] // lax.axis_size("pipe")

    def columns(x, index):
        return lax.dynamic_slice_in_dim(x, index * half_cols, half_cols, 1)

    first_rows = group_rows * 2 // 3 // 16 * 16
    cuts = [(0, first_rows), (first_rows, group_rows)]
    out_right = passed_along(jnp.concatenate([main_out[0], key_rows[-16:]], 0), "seq", 1)
    out_left = passed_along(jnp.concatenate([main_out[0], query_rows[:16]], 0), "seq", -1)
    query_other = swapped(query_rows, "groups")
    key_other = swapped(key_rows, "groups")
    own_weights = []
    for low, high in cuts:
        piece = jnp.concatenate(
            [
                lax.dynamic_slice(
                    weight,
                    (group_index * group_rows + low, pipe_index * half_cols),
                    (high - low, half_cols),
                )
                for weight in (query_weight, key_weight)
            ],
            1,
        )
        if own_weights:
            piece = after(piece, out_right)
        own_weights.append(lax.all_gather(piece, "seq", axis=0, tiled=True))
    out_far_right, out_far_left = second_neighbours(out_right, out_left)
    last_key, next_query = out_right[-1:], out_left[span_rows : span_rows + 1]
    edges_other = swapped(jnp.concatenate([last_key, next_query], 0), "groups")
    last_key_other, next_query_other = edges_other[:1], edges_other[1:]
    blocks = [out_far_right, out_right, main_out[0], out_left, out_far_left]
    sums = byte_sums(shard_index, boundaries, cotangent, query_rows, key_rows, blocks)

    positions = shard_index * row_count + jnp.arange(row_count, dtype=jnp.int32)
    span_of = jnp.sum((bounds_row[None, :] <= positions[:, None]).astype(jnp.int32), 1) - 1
    starts = jnp.any(bounds_row[None, :] == positions[:, None], 1)
    place = span_of - (shard_index - reach) * span_rows
    window_rows = (2 * reach + 1) * span_rows
    selector = place[:, None] == jnp.arange(window_rows, dtype=jnp.int32)[None, :]
    cotangent_wide = cotangent.astype(jnp.float32)
    if tensor_count == 2:
        sums = sums + swapped(sums, "tensor")
    else:
        sums = lax.psum(sums, "tensor")
    cross_sum, query_sum, key_sum, conf_grad = sums[:4]
    query_scale = lax.rsqrt(query_sum + epsilon)
    key_scale = lax.rsqrt(key_sum + epsilon)
    cosine = cross_sum * query_scale * key_scale
    probability = jnp.where(positions == 0, 1.0, 0.5 * (1.0 - cosine))
    confidence = jnp.where(starts, probability, 1.0 - probability)
    sign = jnp.where(starts, 1.0, -1.0)
    cos_grad = jnp.where(positions == 0, 0.0, -0.5 * sign * conf_grad)
    factors = jnp.stack(
        [
            cos_grad * (query_scale * key_scale),
            cos_grad * (cosine * query_scale * query_scale),
            cos_grad * (cosine * key_scale * key_scale),
        ]
    )
    next_factors = passed_along(factors[:, :1], "seq", -1)
    factors = jnp.concatenate([factors, next_factors], 1)
    factors_other = swapped(factors, "groups")

    def grads(queries_here, keys_here, key_before, query_after, here, index):
        previous = jnp.concatenate([columns(key_before, index), columns(keys_here, index)[:-1]], 0)
        current = columns(queries_here, index)
        following = jnp.concatenate([current[1:], columns(query_after, index)], 0)
        ahead, here = here[:, 1:], here[:, :-1]
        query_grad = here[0][:, None] * previous.astype(jnp.float32)
        query_grad = query_grad - here[1][:, None] * current.astype(jnp.float32)
        key_grad = ahead[0][:, None] * following.astype(jnp.float32)
        key_grad = key_grad - ahead[2][:, None] * columns(keys_here, index).astype(jnp.float32)
        return jnp.concatenate([query_grad.astype(jnp.bfloat16), key_grad.astype(jnp.bfloat16)], 1)

    def both_grads(index):
        own = grads(query_rows, key_rows, last_key, next_query, factors, index)
        other = grads(
            query_other,
            key_other,
            last_key_other,
            next_query_other,
            factors_other,
            index,
        )
        return jnp.concatenate([own, other], 0)

    own_side, other_side = both_grads(pipe_index), both_grads(1 - pipe_index)

    def span_part(ready):
        conf_high = confidence.astype(jnp.bfloat16)
        conf_low = (confidence - conf_high.astype(jnp.float32)).astype(jnp.bfloat16)
        zero_weight = jnp.zeros((), jnp.bfloat16)
        weight_high = jnp.where(selector, conf_high[:, None], zero_weight)
        weight_low = jnp.where(selector, conf_low[:, None], zero_weight)
        contract = (((0,), (0,)), ((), ()))
        span_terms = lax.dot_general(
            weight_high, cotangent, contract, preferred_element_type=jnp.float32
        )
        span_terms = span_terms + lax.dot_general(
            weight_low, cotangent, contract, preferred_element_type=jnp.float32
        )
        terms = [span_terms[i * span_rows : (i + 1) * span_rows] for i in range(2 * reach + 1)]

        def moved(block, by, further):
            moved_block = passed_on(block.astype(jnp.bfloat16), "seq", by, further)
            return moved_block.astype(jnp.float32)

        outer = after(jnp.stack([terms[0], terms[4]]).astype(jnp.bfloat16), ready)
        inner = jnp.stack(
            [terms[1] + moved(outer[0], -1, -2), terms[3] + moved(outer[1], 1, 2)]
        )
        return terms[reach], inner.astype(jnp.bfloat16)

    window_grad = lax.all_gather(
        after(main_in_grad[0], own_weights[0]), "seq", axis=0, tiled=True
    )
    span_index = jnp.arange(window_grad.shape[0], dtype=jnp.int32)
    start_picker = ((span_of[:, None] == span_index[None, :]) & starts[:, None]).astype(jnp.bfloat16)
    start_grad = jnp.dot(start_picker, window_grad, preferred_element_type=jnp.float32)

    def partial(own_weight, other_weight):
        total = product(own_side, own_weight) + product(other_side, other_weight)
        return total.astype(jnp.bfloat16)

    pieces = []
    span_sums, span_inner = span_part(factors_other)
    far_part = None
    for own_weight in own_weights:
        if far_part is not None:
            own_weight = after(own_weight, far_part)
        other_weight = swapped(own_weight, "pipe")
        block_rows = own_weight.shape[0] // tensor_count
        if tensor_count == 2:

            def half(index):
                return [
                    lax.dynamic_slice_in_dim(weight, index * block_rows, block_rows, 0)
                    for weight in (own_weight, other_weight)
                ]

            far_part = partial(*half(1 - tensor_index))
            incoming = swapped(far_part, "tensor").astype(jnp.float32)
            total = partial(*half(tensor_index)).astype(jnp.float32) + incoming
        else:
            far_part = partial(own_weight, other_weight)
            total = lax.psum_scatter(
                far_part, "tensor", scatter_dimension=1, tiled=True
            ).astype(jnp.float32)
        own = total[:row_count]
        returned = total[row_count:].astype(jnp.bfloat16)
        arrived = swapped(returned, "groups").astype(jnp.float32)
        pieces.append(
            [jnp.where(group_index == 0, own, arrived), jnp.where(group_index == 0, arrived, own)]
        )
    span_inner = after(span_inner, far_part)
    span_sums = span_sums + passed_along(span_inner[0], "seq", -1).astype(jnp.float32)
    span_sums = span_sums + passed_along(span_inner[1], "seq", 1).astype(jnp.float32)
    main_grad = span_sums.astype(jnp.bfloat16)[None]
    widths = [high - low for low, high in cuts]
    routing = jnp.concatenate(
        [
            piece[group][:, s * width : (s + 1) * width]
            for s in range(seq_count // tensor_count)
            for group in range(2)
            for piece, width in zip(pieces, widths)
        ],
        1,
    )
    byte_grad = (cotangent_wide + start_grad + routing).astype(jnp.bfloat16)[None]
    return (byte_grad, main_grad)


def solution(mesh):
    return jax.shard_map(
        shards,
        mesh=mesh,
        in_specs=(
            P(("groups", "pipe"), "seq", "tensor"),
            P(("groups", "pipe"), "seq", "tensor"),
            P(("groups", "pipe"), "seq", "tensor"),
            P(("groups", "pipe"), "seq", "tensor"),
            P(("groups", "pipe"), "seq", "tensor"),
            P(("groups", "pipe"), None),
            P("seq", "tensor"),
            P("seq", "tensor"),
        ),
        out_specs=(P(("groups", "pipe"), "seq", "tensor"), P(("groups", "pipe"), "seq", "tensor")),
        check_vma=False,
    )
```

```python
import jax
import jax.numpy as jnp
from jax import lax
from jax.experimental import pallas as pl
from jax.experimental.pallas import tpu as pltpu
from jax.sharding import PartitionSpec as P

epsilon = 1e-06


def passed_along(x, axis, by):
    length = lax.axis_size(axis)
    pairs = [(i, i + by) for i in range(length) if 0 <= i + by < length]
    return lax.ppermute(x, axis, pairs)


reach = 2


def swapped(x, axis):
    length = lax.axis_size(axis)
    return lax.ppermute(x, axis, [(i, length - 1 - i) for i in range(length)])


def passed_on(x, axis, by, came_from):
    length = lax.axis_size(axis)
    pairs = [
        (i, i + by) for i in range(length) if 0 <= i + by < length and 0 <= i + came_from < length
    ]
    return lax.ppermute(x, axis, pairs)


def second_neighbours(right, left):
    return passed_on(right, "seq", 1, -1), passed_on(left, "seq", -1, 1)


def after(value, *others):
    def kernel(*refs):
        del refs

    anywhere = pl.BlockSpec(memory_space=pl.ANY)
    return pl.pallas_call(
        kernel,
        out_shape=jax.ShapeDtypeStruct(value.shape, value.dtype),
        in_specs=[anywhere] * (1 + len(others)),
        out_specs=anywhere,
        input_output_aliases={0: 0},
        name="after",
    )(value, *others)


def byte_sums_kernel(shard_ref, bounds_ref, cotangent_ref, query_ref, key_ref, *refs):
    blocks, out_ref = refs[:-1], refs[-1]
    rows, width = query_ref.shape
    span_rows = blocks[reach].shape[0]
    shard = shard_ref[0]
    row = lax.broadcasted_iota(jnp.int32, (rows, 1), 0)
    held = (bounds_ref[...] <= shard * rows + row).astype(jnp.float32)
    span_of = jnp.sum(held, 1, keepdims=True).astype(jnp.int32) - 1
    place = span_of - (shard - reach) * span_rows
    column = lax.broadcasted_iota(jnp.int32, (rows, span_rows), 1)
    pickers = [
        (place - i * span_rows == column).astype(jnp.float32).astype(jnp.bfloat16)
        for i in range(len(blocks))
    ]
    last_row = blocks[reach - 1].shape[0] - 1
    tile = 384
    totals = [jnp.zeros((rows, 128), jnp.float32)] * 4
    for start in range(0, width, tile):
        cols = pl.ds(start, tile)
        upsampled = jnp.zeros((rows, tile), jnp.float32)
        for picker, block in zip(pickers, blocks):
            upsampled = upsampled + jnp.dot(
                picker, block[:span_rows, cols], preferred_element_type=jnp.float32
            )
        query = query_ref[:, cols].astype(jnp.float32)
        previous = pltpu.roll(key_ref[:, cols].astype(jnp.float32), 1, 0)
        edge = blocks[reach - 1][last_row - 15 :, cols].astype(jnp.float32)[15:16]
        previous = jnp.where(row == 0, edge, previous)
        cotangent = cotangent_ref[:, cols].astype(jnp.float32)
        terms = [query * previous, query * query, previous * previous, cotangent * upsampled]
        for piece in range(0, tile, 128):
            totals = [
                total + term[:, piece : piece + 128] for total, term in zip(totals, terms)
            ]
    lines = [jnp.sum(total.T, 0, keepdims=True) for total in totals]
    out_ref[...] = jnp.concatenate(lines + [jnp.zeros((4, rows), jnp.float32)], 0)


def byte_sums(shard_index, bounds, cotangent, query_rows, key_rows, blocks):
    rows = query_rows.shape[0]
    vmem = pl.BlockSpec(memory_space=pltpu.VMEM)
    return pl.pallas_call(
        byte_sums_kernel,
        out_shape=jax.ShapeDtypeStruct((8, rows), jnp.float32),
        in_specs=[pl.BlockSpec(memory_space=pltpu.SMEM)] + [vmem] * (4 + len(blocks)),
        out_specs=vmem,
        compiler_params=pltpu.CompilerParams(vmem_limit_bytes=40 * 1024 * 1024),
        name="byte_sums",
    )(shard_index[None], bounds, cotangent, query_rows, key_rows, *blocks)


def product(rows, weight):
    return lax.dot_general(
        rows, weight, (((1,), (1,)), ((), ())), preferred_element_type=jnp.float32
    )


def shards(out_grad, queries, keys, main_out, main_in_grad, boundaries, query_weight, key_weight):
    cotangent = out_grad[0]
    query_rows = queries[0]
    key_rows = keys[0]
    bounds_row = boundaries[0]
    row_count = cotangent.shape[0]
    span_rows = main_out.shape[1]
    shard_index = lax.axis_index("seq")
    seq_count = lax.axis_size("seq")
    tensor_count = lax.axis_size("tensor")
    tensor_index = lax.axis_index("tensor")
    group_index = lax.axis_index("groups")
    pipe_index = lax.axis_index("pipe")
    group_rows = query_weight.shape[0] // lax.axis_size("groups")
    half_cols = query_weight.shape[1] // lax.axis_size("pipe")

    def columns(x, index):
        return lax.dynamic_slice_in_dim(x, index * half_cols, half_cols, 1)

    first_rows = group_rows * 2 // 3 // 16 * 16
    cuts = [(0, first_rows), (first_rows, group_rows)]
    out_right = passed_along(jnp.concatenate([main_out[0], key_rows[-16:]], 0), "seq", 1)
    out_left = passed_along(jnp.concatenate([main_out[0], query_rows[:16]], 0), "seq", -1)
    query_other = swapped(query_rows, "groups")
    key_other = swapped(key_rows, "groups")
    own_weights = []
    for low, high in cuts:
        piece = jnp.concatenate(
            [
                lax.dynamic_slice(
                    weight,
                    (group_index * group_rows + low, pipe_index * half_cols),
                    (high - low, half_cols),
                )
                for weight in (query_weight, key_weight)
            ],
            1,
        )
        if own_weights:
            piece = after(piece, out_right)
        own_weights.append(lax.all_gather(piece, "seq", axis=0, tiled=True))
    out_far_right, out_far_left = second_neighbours(out_right, out_left)
    last_key, next_query = out_right[-1:], out_left[span_rows : span_rows + 1]
    edges_other = swapped(jnp.concatenate([last_key, next_query], 0), "groups")
    last_key_other, next_query_other = edges_other[:1], edges_other[1:]
    blocks = [out_far_right, out_right, main_out[0], out_left, out_far_left]
    sums = byte_sums(shard_index, boundaries, cotangent, query_rows, key_rows, blocks)

    positions = shard_index * row_count + jnp.arange(row_count, dtype=jnp.int32)
    span_of = jnp.sum((bounds_row[None, :] <= positions[:, None]).astype(jnp.int32), 1) - 1
    starts = jnp.any(bounds_row[None, :] == positions[:, None], 1)
    place = span_of - (shard_index - reach) * span_rows
    window_rows = (2 * reach + 1) * span_rows
    selector = place[:, None] == jnp.arange(window_rows, dtype=jnp.int32)[None, :]
    cotangent_wide = cotangent.astype(jnp.float32)
    if tensor_count == 2:
        sums = sums + swapped(sums, "tensor")
    else:
        sums = lax.psum(sums, "tensor")
    cross_sum, query_sum, key_sum, conf_grad = sums[:4]
    query_scale = lax.rsqrt(query_sum + epsilon)
    key_scale = lax.rsqrt(key_sum + epsilon)
    cosine = cross_sum * query_scale * key_scale
    probability = jnp.where(positions == 0, 1.0, 0.5 * (1.0 - cosine))
    confidence = jnp.where(starts, probability, 1.0 - probability)
    sign = jnp.where(starts, 1.0, -1.0)
    cos_grad = jnp.where(positions == 0, 0.0, -0.5 * sign * conf_grad)
    factors = jnp.stack(
        [
            cos_grad * (query_scale * key_scale),
            cos_grad * (cosine * query_scale * query_scale),
            cos_grad * (cosine * key_scale * key_scale),
        ]
    )
    next_factors = passed_along(factors[:, :1], "seq", -1)
    factors = jnp.concatenate([factors, next_factors], 1)
    factors_other = swapped(factors, "groups")

    def grads(queries_here, keys_here, key_before, query_after, here, index):
        previous = jnp.concatenate([columns(key_before, index), columns(keys_here, index)[:-1]], 0)
        current = columns(queries_here, index)
        following = jnp.concatenate([current[1:], columns(query_after, index)], 0)
        ahead, here = here[:, 1:], here[:, :-1]
        query_grad = here[0][:, None] * previous.astype(jnp.float32)
        query_grad = query_grad - here[1][:, None] * current.astype(jnp.float32)
        key_grad = ahead[0][:, None] * following.astype(jnp.float32)
        key_grad = key_grad - ahead[2][:, None] * columns(keys_here, index).astype(jnp.float32)
        return jnp.concatenate([query_grad.astype(jnp.bfloat16), key_grad.astype(jnp.bfloat16)], 1)

    def both_grads(index):
        own = grads(query_rows, key_rows, last_key, next_query, factors, index)
        other = grads(
            query_other,
            key_other,
            last_key_other,
            next_query_other,
            factors_other,
            index,
        )
        return jnp.concatenate([own, other], 0)

    own_side, other_side = both_grads(pipe_index), both_grads(1 - pipe_index)

    def span_part(ready):
        conf_high = confidence.astype(jnp.bfloat16)
        conf_low = (confidence - conf_high.astype(jnp.float32)).astype(jnp.bfloat16)
        zero_weight = jnp.zeros((), jnp.bfloat16)
        weight_high = jnp.where(selector, conf_high[:, None], zero_weight)
        weight_low = jnp.where(selector, conf_low[:, None], zero_weight)
        contract = (((0,), (0,)), ((), ()))
        span_terms = lax.dot_general(
            weight_high, cotangent, contract, preferred_element_type=jnp.float32
        )
        span_terms = span_terms + lax.dot_general(
            weight_low, cotangent, contract, preferred_element_type=jnp.float32
        )
        terms = [span_terms[i * span_rows : (i + 1) * span_rows] for i in range(2 * reach + 1)]

        def moved(block, by, further):
            moved_block = passed_on(block.astype(jnp.bfloat16), "seq", by, further)
            return moved_block.astype(jnp.float32)

        outer = after(jnp.stack([terms[0], terms[4]]).astype(jnp.bfloat16), ready)
        span_sums = terms[2] + moved(terms[3] + moved(outer[1], 1, 2), 1, 1)
        span_sums = span_sums + moved(terms[1] + moved(outer[0], -1, -2), -1, -1)
        return span_sums.astype(jnp.bfloat16)[None]

    window_grad = lax.all_gather(
        after(main_in_grad[0], own_weights[0]), "seq", axis=0, tiled=True
    )
    span_index = jnp.arange(window_grad.shape[0], dtype=jnp.int32)
    start_picker = ((span_of[:, None] == span_index[None, :]) & starts[:, None]).astype(jnp.bfloat16)
    start_grad = jnp.dot(start_picker, window_grad, preferred_element_type=jnp.float32)

    def partial(own_weight, other_weight):
        total = product(own_side, own_weight) + product(other_side, other_weight)
        return total.astype(jnp.bfloat16)

    pieces = []
    main_grad = span_part(sums)
    far_part = None
    for own_weight in own_weights:
        if far_part is not None:
            own_weight = after(own_weight, far_part)
        other_weight = swapped(own_weight, "pipe")
        block_rows = own_weight.shape[0] // tensor_count
        if tensor_count == 2:

            def half(index):
                return [
                    lax.dynamic_slice_in_dim(weight, index * block_rows, block_rows, 0)
                    for weight in (own_weight, other_weight)
                ]

            far_part = partial(*half(1 - tensor_index))
            incoming = swapped(far_part, "tensor").astype(jnp.float32)
            total = partial(*half(tensor_index)).astype(jnp.float32) + incoming
        else:
            total = lax.psum_scatter(
                partial(own_weight, other_weight), "tensor", scatter_dimension=1, tiled=True
            ).astype(jnp.float32)
        own = total[:row_count]
        returned = total[row_count:].astype(jnp.bfloat16)
        arrived = swapped(returned, "groups").astype(jnp.float32)
        pieces.append(
            [jnp.where(group_index == 0, own, arrived), jnp.where(group_index == 0, arrived, own)]
        )
    widths = [high - low for low, high in cuts]
    routing = jnp.concatenate(
        [
            piece[group][:, s * width : (s + 1) * width]
            for s in range(seq_count // tensor_count)
            for group in range(2)
            for piece, width in zip(pieces, widths)
        ],
        1,
    )
    byte_grad = (cotangent_wide + start_grad + routing).astype(jnp.bfloat16)[None]
    return (byte_grad, main_grad)


def solution(mesh):
    return jax.shard_map(
        shards,
        mesh=mesh,
        in_specs=(
            P(("groups", "pipe"), "seq", "tensor"),
            P(("groups", "pipe"), "seq", "tensor"),
            P(("groups", "pipe"), "seq", "tensor"),
            P(("groups", "pipe"), "seq", "tensor"),
            P(("groups", "pipe"), "seq", "tensor"),
            P(("groups", "pipe"), None),
            P("seq", "tensor"),
            P("seq", "tensor"),
        ),
        out_specs=(P(("groups", "pipe"), "seq", "tensor"), P(("groups", "pipe"), "seq", "tensor")),
        check_vma=False,
    )
```
